512 devices in a mesh: dp: 4 (over x), seq: 128 (over z, y, core).
Axes of the slice: x: 4, y: 4, z: 16, core: 2. Of those that a mesh axis runs over, the one named last changes fastest.
Arguments:
- spatial_query: bfloat16 [4, 128, 128, 576], P('dp', 'seq'), may hold values from -6 to 6
- spatial_key: bfloat16 [4, 128, 128, 576], P('dp', 'seq'), may hold values from -6 to 6
- spatial_value: bfloat16 [4, 128, 128, 576], P('dp', 'seq'), may hold values from -6 to 6
- temporal_query: bfloat16 [4, 128, 128, 576], P('dp', 'seq'), may hold values from -6 to 6
- temporal_key: bfloat16 [4, 128, 128, 576], P('dp', 'seq'), may hold values from -6 to 6
- temporal_value_in: bfloat16 [4, 128, 128, 576], P('dp', 'seq'), may hold values from -6 to 6
- out_grad: bfloat16 [4, 128, 128, 576], P('dp', 'seq'), may hold values from -6 to 6
- video_ids: int32 [4, 128], P('dp'), may hold values from 0 to 5, never falling along the last dimension, each value on 1 to 51 neighbouring positions
- spatial_query_gain: float32 [72], replicated, may hold values from 0.5 to 2
- spatial_key_gain: float32 [72], replicated, may hold values from 0.5 to 2
- temporal_query_gain: float32 [72], replicated, may hold values from 0.5 to 2
- temporal_key_gain: float32 [72], replicated, may hold values from 0.5 to 2
Outputs:
- temporal_out: bfloat16 [4, 128, 128, 576], P('dp', 'seq')
- grad_spatial_query: bfloat16 [4, 128, 128, 576], P('dp', 'seq')
- grad_spatial_key: bfloat16 [4, 128, 128, 576], P('dp', 'seq')
- grad_spatial_value: bfloat16 [4, 128, 128, 576], P('dp', 'seq')
- grad_temporal_query: bfloat16 [4, 128, 128, 576], P('dp', 'seq')
- grad_temporal_key: bfloat16 [4, 128, 128, 576], P('dp', 'seq')
- grad_temporal_value_in: bfloat16 [4, 128, 128, 576], P('dp', 'seq')
- grad_spatial_query_gain: float32 [72], replicated
- grad_spatial_key_gain: float32 [72], replicated
- grad_temporal_query_gain: float32 [72], replicated
- grad_temporal_key_gain: float32 [72], replicated
The draws below stay inside these ranges and needn't reach their ends.
Inputs may be any that keep to these rules, and one draw needn't show every extreme that they name: `video_ids`: ids never fall along the frames; each video has 1 to 51 frames.
All inputs are finite; a program needn't handle non-finite values.
Results may differ from the reference program's by a relative error of at most 0.02.
Values may be sent and summed in bfloat16 or wider, within the bound.
No kernel may reach another device: no remote copies, remote signals or barrier semaphores. Data moves between devices by JAX's collectives and lax.ppermute only.
A program may use at most 64 MiB of HBM per device.

```python
import math
import jax
import jax.numpy as jnp
import numpy as np
from jax import lax

HEADS = 8
HEAD_DIM = 72
POS = 128
INNER = 576
FRAMES = 128
MOST_FR = 51
VIDEOS = 6
N_DP = 4


def steps_of(key, extent, shards, low, high):
    def one(position, parts):
        heights = jax.random.uniform(jax.random.fold_in(jax.random.fold_in(key, 6), position), (parts,), jnp.float32, low / len(shards), high / len(shards))
        return jnp.repeat(jnp.exp(heights), extent[position] // parts).reshape((-1,) + (1,) * (len(extent) - position - 1))

    level = one(*shards[0])
    for cut in shards[1:]:
        level = level * one(*cut)
    return level


def length_profile(number_of, total, limit, slope):
    portions = [(1 << 20) // math.isqrt(standing ** slope) + 1 for standing in range(2, number_of + 1)]
    surplus, counts = total - limit - (number_of - 1), [1] * (number_of - 1)
    while surplus > 0:
        free = [i for i in range(number_of - 1) if counts[i] < limit]
        mass, left = sum([portions[i] for i in free]), surplus
        for i in free:
            addition = min(limit - counts[i], max(1, left * portions[i] // mass), surplus)
            counts[i] = counts[i] + addition
            surplus = surplus - addition
    return np.array([limit] + counts)


def ragged_sizes(stream_key, number_of, total, limit, slope):
    if number_of == 2:
        one = jax.random.randint(stream_key, (), max(1, total - limit), min(limit, total - 1) + 1)
        return jnp.stack([one, total - one])
    lengths = jnp.asarray(length_profile(number_of, total, limit, slope), jnp.int32)
    couples = (number_of - 1) // 2
    giver, sink = lengths[1:1 + 2 * couples:2], lengths[2:2 + 2 * couples:2]
    slack = jnp.minimum(giver - 1, limit - sink)
    moved = jax.random.randint(jax.random.fold_in(stream_key, 1), (couples,), 0, 1 << 20) % (slack + 1)
    lengths = lengths.at[1:1 + 2 * couples:2].set(giver - moved).at[2:2 + 2 * couples:2].set(sink + moved)
    return lengths[jax.random.permutation(jax.random.fold_in(stream_key, 2), number_of)]


def normal_values(own_key, extent, width, limit, pieces=(), dtype=jnp.bfloat16):
    level = steps_of(own_key, extent, pieces, -0.22, 0.18) if pieces else 1.0
    values = jax.random.normal(own_key, extent, jnp.float32) * width * level
    return jnp.minimum(jnp.maximum(values, -limit), limit).astype(dtype)


def setup_inputs(seed: int = 0) -> dict:
    key_list = jax.random.split(jax.random.key(seed), 13)
    spatial_query = normal_values(key_list[0], (N_DP, FRAMES, POS, INNER), 1.0, 6.0, ((0, 4), (1, 128)))
    spatial_key = normal_values(key_list[1], (N_DP, FRAMES, POS, INNER), 1.0, 6.0, ((0, 4), (1, 128)))
    spatial_value = normal_values(key_list[2], (N_DP, FRAMES, POS, INNER), 1.0, 6.0, ((0, 4), (1, 128)))
    temporal_query = normal_values(key_list[3], (N_DP, FRAMES, POS, INNER), 1.0, 6.0, ((0, 4), (1, 128)))
    temporal_key = normal_values(key_list[4], (N_DP, FRAMES, POS, INNER), 1.0, 6.0, ((0, 4), (1, 128)))
    temporal_value_in = normal_values(key_list[5], (N_DP, FRAMES, POS, INNER), 1.0, 6.0, ((0, 4), (1, 128)))
    out_grad = normal_values(key_list[6], (N_DP, FRAMES, POS, INNER), 1.0, 6.0, ((0, 4), (1, 128)))
    video_ids = jax.vmap(lambda own: jnp.searchsorted(jnp.cumsum(ragged_sizes(own, VIDEOS, FRAMES, MOST_FR, 1)), jnp.arange(FRAMES), side="right"))(jax.random.split(key_list[7], N_DP)).reshape((N_DP, FRAMES)).astype(jnp.int32)
    spatial_query_gain = jnp.clip(jnp.exp(jax.random.uniform(key_list[8], (HEAD_DIM,), jnp.float32, math.log(0.5), math.log(2.0))), 0.5, 2.0)
    spatial_key_gain = jnp.clip(jnp.exp(jax.random.uniform(key_list[9], (HEAD_DIM,), jnp.float32, math.log(0.5), math.log(2.0))), 0.5, 2.0)
    temporal_query_gain = jnp.clip(jnp.exp(jax.random.uniform(key_list[10], (HEAD_DIM,), jnp.float32, math.log(0.5), math.log(2.0))), 0.5, 2.0)
    temporal_key_gain = jnp.clip(jnp.exp(jax.random.uniform(key_list[11], (HEAD_DIM,), jnp.float32, math.log(0.5), math.log(2.0))), 0.5, 2.0)
    return {"spatial_query": spatial_query, "spatial_key": spatial_key, "spatial_value": spatial_value, "temporal_query": temporal_query, "temporal_key": temporal_key, "temporal_value_in": temporal_value_in, "out_grad": out_grad, "video_ids": video_ids, "spatial_query_gain": spatial_query_gain, "spatial_key_gain": spatial_key_gain, "temporal_query_gain": temporal_query_gain, "temporal_key_gain": temporal_key_gain}


def normed(values, gain):
    floats = values.astype(jnp.float32)
    square = lax.optimization_barrier(jnp.mean(floats * floats, axis=-1, keepdims=True))
    return (floats * lax.rsqrt(square + 1e-06) * gain).astype(jnp.bfloat16)

def attend(query, key_in, value, query_gain, key_gain, penalty, score_form, mix_form):
    shape = query.shape
    split = shape[:-1] + (HEADS, HEAD_DIM)
    query_h = normed(query.reshape(split), query_gain)
    key_h = normed(key_in.reshape(split), key_gain)
    value_h = value.reshape(split)
    scores = jnp.einsum(score_form, query_h.astype(jnp.float32), key_h.astype(jnp.float32)) * HEAD_DIM ** (-0.5) + penalty
    probs = jax.nn.softmax(scores, axis=-1).astype(jnp.bfloat16)
    mixed = jnp.einsum(mix_form, probs.astype(jnp.float32), value_h.astype(jnp.float32))
    return mixed.astype(jnp.bfloat16).reshape(shape)

def block_pair(penalty, sq, sk, sv, tq, tk, tv_in, gain_a, gain_b, gain_c, gain_d):
    spatial_out = attend(sq, sk, sv, gain_a, gain_b, jnp.float32(0.0), 'fqhe,fkhe->fhqk', 'fhqk,fkhe->fqhe')
    temporal_value = (tv_in.astype(jnp.float32) + spatial_out.astype(jnp.float32)).astype(jnp.bfloat16)
    return attend(tq, tk, temporal_value, gain_c, gain_d, penalty, 'qphe,kphe->phqk', 'phqk,kphe->qphe')

def reference(spatial_query, spatial_key, spatial_value, temporal_query, temporal_key, temporal_value_in, out_grad, video_ids, spatial_query_gain, spatial_key_gain, temporal_query_gain, temporal_key_gain):
    gains = (spatial_query_gain, spatial_key_gain, temporal_query_gain, temporal_key_gain)

    def one_pack(packed):
        sq, sk, sv, tq, tk, tv_in, cotan, ids = packed
        penalty = jnp.where(ids[:, None] == ids[None, :], 0.0, -1000000000.0).astype(jnp.float32)
        result, pullback = jax.vjp(partial_pair(penalty), sq, sk, sv, tq, tk, tv_in, *gains)
        return (result,) + tuple(pullback(cotan))
    outputs = lax.map(one_pack, (spatial_query, spatial_key, spatial_value, temporal_query, temporal_key, temporal_value_in, out_grad, video_ids))
    gain_grads = tuple((lax.optimization_barrier(jnp.sum(outputs[7 + index].astype(jnp.float32), axis=0)) for index in range(4)))
    return (outputs[0], outputs[1], outputs[2], outputs[3], outputs[4], outputs[5], outputs[6], gain_grads[0], gain_grads[1], gain_grads[2], gain_grads[3])

def partial_pair(penalty):

    def inner(*arrays):
        return block_pair(penalty, *arrays)
    return inner
```

```python
import jax
import jax.numpy as jnp
from jax import lax
from jax.experimental import pallas as pl
from jax.experimental.pallas import tpu as pltpu
from jax.sharding import Mesh
from jax.sharding import PartitionSpec as P

HEADS = 8
HEAD_DIM = 72
INNER = 576
TOKENS = 128
SCALE = HEAD_DIM ** (-0.5)
EPS = 1e-06
BF = jnp.bfloat16
F32 = jnp.float32
PARAMS = pltpu.CompilerParams(vmem_limit_bytes=48 * 1024 * 1024)


def dot(left, right, left_dim, right_dim):
    return lax.dot_general(
        left, right, (((left_dim,), (right_dim,)), ((), ())), preferred_element_type=F32
    )


def pack(features, tiles, out_ref):
    size = 16 * tiles
    row = lax.broadcasted_iota(jnp.int32, (size, size), 0)
    col = lax.broadcasted_iota(jnp.int32, (size, size), 1)
    order = (row == (col & 15) * tiles + (col >> 4)).astype(F32).astype(BF)
    stacked = []
    for tile in range(tiles):
        turned = features[128 * tile : 128 * tile + 128, :].T
        stacked.append(
            jnp.concatenate([turned[16 * b : 16 * b + 16, :] for b in range(8)], axis=1)
        )
    mixed = dot(order, jnp.concatenate(stacked, axis=0), 1, 0).astype(BF)
    for b in range(8):
        out_ref[size * b : size * b + size, :] = mixed[:, 128 * b : 128 * b + 128]


def unpack(in_ref, tiles):
    size = 16 * tiles
    row = lax.broadcasted_iota(jnp.int32, (size, size), 0)
    col = lax.broadcasted_iota(jnp.int32, (size, size), 1)
    order = (col == (row & 15) * tiles + (row >> 4)).astype(F32).astype(BF)
    blocks = jnp.concatenate(
        [in_ref[size * b : size * b + size, :] for b in range(8)], axis=1
    )
    mixed = dot(order, blocks, 1, 0).astype(BF)
    turned = []
    for tile in range(tiles):
        rows = mixed[16 * tile : 16 * tile + 16, :]
        turned.append(
            jnp.concatenate([rows[:, 128 * b : 128 * b + 128] for b in range(8)], axis=0).T
        )
    return jnp.concatenate(turned, axis=0)


def column(gain_ref):
    row = lax.broadcasted_iota(jnp.int32, (HEAD_DIM, HEAD_DIM), 0)
    col = lax.broadcasted_iota(jnp.int32, (HEAD_DIM, HEAD_DIM), 1)
    spread = jnp.where(row == col, gain_ref[...], 0.0)
    return jnp.sum(spread, axis=1, keepdims=True)


def normed(values, gain):
    floats = values.astype(F32).reshape(HEADS, HEAD_DIM, TOKENS)
    inverse = lax.rsqrt(jnp.mean(floats * floats, axis=1, keepdims=True) + EPS)
    unit = floats * inverse
    return unit, inverse, (unit * gain[None]).astype(BF)


def normed_back(cotangent, unit, inverse, gain):
    scaled = cotangent * gain[None]
    along = jnp.mean(scaled * unit, axis=1, keepdims=True)
    grad = inverse * (scaled - unit * along)
    return grad.reshape(INNER, TOKENS).astype(BF), jnp.sum(cotangent * unit, axis=0)


def probabilities(query, key_in, same):
    weights = jnp.exp(dot(key_in, query, 0, 0) * SCALE)
    if same is not None:
        weights = weights * same
    return weights * (1.0 / jnp.sum(weights, axis=0, keepdims=True))


def attention_back(probs, query, key_in, value, cotangent):
    rounded = probs.astype(BF)
    grad_value = dot(cotangent, rounded, 1, 1)
    grad_probs = dot(value, cotangent, 0, 0)
    along = jnp.sum(probs * grad_probs, axis=0, keepdims=True)
    grad_scores = (probs * (grad_probs - along) * SCALE).astype(BF)
    grad_query = dot(key_in, grad_scores, 1, 0)
    grad_key = dot(query, grad_scores, 1, 1)
    return grad_query, grad_key, grad_value


def head(values, index):
    return values[HEAD_DIM * index : HEAD_DIM * (index + 1), :]


def by_head(parts):
    return jnp.stack([part.astype(BF).astype(F32) for part in parts])


def gain_row(terms):
    return jnp.sum(terms.T, axis=0, keepdims=True)


def send_kernel(sq, sk, sv, tq, tk, tv_in, og, gain_q, gain_k, out_ref):
    _, _, query = normed(sq[...], column(gain_q))
    _, _, key_in = normed(sk[...], column(gain_k))
    value = sv[...]
    mixed = []
    for h in range(HEADS):
        probs = probabilities(query[h], key_in[h], None).astype(BF)
        mixed.append(dot(head(value, h), probs, 1, 0))
    spatial = jnp.concatenate(mixed, axis=0).astype(BF)
    total = (tv_in[...].astype(F32) + spatial.astype(F32)).astype(BF)
    pack(jnp.concatenate([tq[...], tk[...], og[...], total], axis=0), 18, out_ref)


def temporal_kernel(in_ref, ids_ref, gain_q, gain_k, out_ref, gains_ref):
    arrays = unpack(in_ref, 18)
    tq, tk, og, tv = (arrays[INNER * i : INNER * (i + 1), :] for i in range(4))
    column_q, column_k = column(gain_q), column(gain_k)
    unit_q, inverse_q, query = normed(tq, column_q)
    unit_k, inverse_k, key_in = normed(tk, column_k)
    ids = jnp.broadcast_to(ids_ref[...].astype(F32), (TOKENS, TOKENS))
    same = (ids == ids.T).astype(F32)
    mixed, grads_q, grads_k, grads_v = [], [], [], []
    for h in range(HEADS):
        probs = probabilities(query[h], key_in[h], same)
        value, cotangent = head(tv, h), head(og, h)
        mixed.append(dot(value, probs.astype(BF), 1, 0))
        grad_q, grad_k, grad_v = attention_back(probs, query[h], key_in[h], value, cotangent)
        grads_q.append(grad_q)
        grads_k.append(grad_k)
        grads_v.append(grad_v)
    out = jnp.concatenate(mixed, axis=0).astype(BF)
    grad_v = jnp.concatenate(grads_v, axis=0).astype(BF)
    grad_q, terms_q = normed_back(by_head(grads_q), unit_q, inverse_q, column_q)
    grad_k, terms_k = normed_back(by_head(grads_k), unit_k, inverse_k, column_k)
    gains_ref[0:1, :] = gain_row(terms_q)
    gains_ref[1:2, :] = gain_row(terms_k)
    pack(jnp.concatenate([out, grad_q, grad_k, grad_v], axis=0), 18, out_ref)


def spatial_back_kernel(
    in_ref, sq, sk, sv, gain_q, gain_k, gains_in, out, grad_tq, grad_tk, grad_tv, grad_sq, grad_sk, grad_sv, gains_ref
):
    arrays = unpack(in_ref, 18)
    out[...], grad_tq[...], grad_tk[...], grad_tv[...] = (
        arrays[INNER * i : INNER * (i + 1), :] for i in range(4)
    )
    given = arrays[INNER * 3 :, :]
    column_q, column_k = column(gain_q), column(gain_k)
    unit_q, inverse_q, query = normed(sq[...], column_q)
    unit_k, inverse_k, key_in = normed(sk[...], column_k)
    value_all = sv[...]
    grads_q, grads_k, grads_v = [], [], []
    for h in range(HEADS):
        probs = probabilities(query[h], key_in[h], None)
        grad_q, grad_k, grad_v = attention_back(
            probs, query[h], key_in[h], head(value_all, h), head(given, h)
        )
        grads_q.append(grad_q)
        grads_k.append(grad_k)
        grads_v.append(grad_v)
    grad_sv[...] = jnp.concatenate(grads_v, axis=0).astype(BF)
    grad_sq[...], terms_q = normed_back(by_head(grads_q), unit_q, inverse_q, column_q)
    grad_sk[...], terms_k = normed_back(by_head(grads_k), unit_k, inverse_k, column_k)
    rows = jnp.concatenate([gain_row(terms_q), gain_row(terms_k), gains_in[...]], axis=0)
    rows = jnp.concatenate([rows, jnp.zeros((4, 128 - HEAD_DIM), F32)], axis=1)
    gains_ref[...] = jnp.broadcast_to(rows[None], gains_ref.shape)


def gain_middle_kernel(in_ref, out_ref):
    out_ref[...] = jnp.broadcast_to(jnp.sum(in_ref[...], axis=0, keepdims=True), out_ref.shape)


def gain_last_kernel(in_ref, *outs):
    total = jnp.sum(in_ref[...], axis=0)
    for i, out in enumerate(outs):
        out[...] = total[i : i + 1, :HEAD_DIM]


def shape(*extent, dtype=BF):
    return jax.ShapeDtypeStruct(extent, dtype)


def exchange(message, axes, tiles):
    parts = message.reshape(TOKENS, tiles // 2, 2, 128)
    parts = lax.all_to_all(parts, axes, split_axis=0, concat_axis=0, tiled=True)
    return parts.reshape(TOKENS * tiles, 128)


def shards(
    spatial_query,
    spatial_key,
    spatial_value,
    temporal_query,
    temporal_key,
    temporal_value_in,
    out_grad,
    video_ids,
    spatial_query_gain,
    spatial_key_gain,
    temporal_query_gain,
    temporal_key_gain,
):
    sq, sk, sv, tq, tk, tv_in, og = (
        a.reshape(TOKENS, INNER).T
        for a in (
            spatial_query,
            spatial_key,
            spatial_value,
            temporal_query,
            temporal_key,
            temporal_value_in,
            out_grad,
        )
    )
    sq_gain, sk_gain, tq_gain, tk_gain = (
        g.reshape(1, HEAD_DIM)
        for g in (spatial_query_gain, spatial_key_gain, temporal_query_gain, temporal_key_gain)
    )
    seq = ("z", "y", "core")
    sent = pl.pallas_call(send_kernel, out_shape=shape(2304, 128), compiler_params=PARAMS)(
        sq, sk, sv, tq, tk, tv_in, og, sq_gain, sk_gain
    )
    arrived = exchange(sent, seq, 18)
    sent, temporal_gains = pl.pallas_call(
        temporal_kernel,
        out_shape=(shape(2304, 128), shape(2, HEAD_DIM, dtype=F32)),
        compiler_params=PARAMS,
    )(arrived, video_ids, tq_gain, tk_gain)
    arrived = exchange(sent, seq, 18)
    results = pl.pallas_call(
        spatial_back_kernel,
        out_shape=(shape(INNER, TOKENS),) * 7 + (shape(16, 4, 128, dtype=F32),),
        compiler_params=PARAMS,
    )(arrived, sq, sk, sv, sq_gain, sk_gain, temporal_gains)
    out, grad_tq, grad_tk, grad_tv, grad_sq, grad_sk, grad_sv, gains = results
    gains = lax.all_to_all(gains, "z", split_axis=0, concat_axis=0, tiled=True)
    gains = pl.pallas_call(
        gain_middle_kernel, out_shape=shape(32, 4, 128, dtype=F32), compiler_params=PARAMS
    )(gains)
    gains = lax.all_to_all(gains, ("dp", "y", "core"), split_axis=0, concat_axis=0, tiled=True)
    gains = pl.pallas_call(
        gain_last_kernel, out_shape=(shape(1, HEAD_DIM, dtype=F32),) * 4, compiler_params=PARAMS
    )(gains)
    arrays = (out, grad_sq, grad_sk, grad_sv, grad_tq, grad_tk, grad_tv)
    return tuple(a.T.reshape(1, 1, TOKENS, INNER) for a in arrays) + tuple(
        g.reshape(HEAD_DIM) for g in gains
    )


def solution(mesh):
    fine = Mesh(mesh.devices.reshape(4, 16, 4, 2), ("dp", "z", "y", "core"))
    tokens = P("dp", ("z", "y", "core"), None, None)
    return jax.shard_map(
        shards,
        mesh=fine,
        in_specs=(tokens,) * 7 + (P("dp", None),) + (P(),) * 4,
        out_specs=(tokens,) * 7 + (P(),) * 4,
        check_vma=False,
    )
```

```python
import jax
import jax.numpy as jnp
from jax import lax
from jax.experimental import pallas as pl
from jax.experimental.pallas import tpu as pltpu
from jax.sharding import Mesh
from jax.sharding import PartitionSpec as P

HEADS = 8
HEAD_DIM = 72
INNER = 576
TOKENS = 128
SCALE = HEAD_DIM ** (-0.5)
EPS = 1e-06
BF = jnp.bfloat16
F32 = jnp.float32
MIB = 1024 * 1024


def dot(left, right, left_dim, right_dim):
    return lax.dot_general(
        left, right, (((left_dim,), (right_dim,)), ((), ())), preferred_element_type=F32
    )


def pack(features, tiles, out_ref):
    size = 16 * tiles
    row = lax.broadcasted_iota(jnp.int32, (size, size), 0)
    col = lax.broadcasted_iota(jnp.int32, (size, size), 1)
    order = (row == (col & 15) * tiles + (col >> 4)).astype(F32).astype(BF)
    stacked = []
    for tile in range(tiles):
        turned = features[128 * tile : 128 * tile + 128, :].T
        stacked.append(
            jnp.concatenate([turned[16 * b : 16 * b + 16, :] for b in range(8)], axis=1)
        )
    mixed = dot(order, jnp.concatenate(stacked, axis=0), 1, 0).astype(BF)
    for b in range(8):
        out_ref[size * b : size * b + size, :] = mixed[:, 128 * b : 128 * b + 128]


def unpack(in_ref, tiles):
    size = 16 * tiles
    row = lax.broadcasted_iota(jnp.int32, (size, size), 0)
    col = lax.broadcasted_iota(jnp.int32, (size, size), 1)
    order = (col == (row & 15) * tiles + (row >> 4)).astype(F32).astype(BF)
    blocks = jnp.concatenate(
        [in_ref[size * b : size * b + size, :] for b in range(8)], axis=1
    )
    mixed = dot(order, blocks, 1, 0).astype(BF)
    turned = []
    for tile in range(tiles):
        rows = mixed[16 * tile : 16 * tile + 16, :]
        turned.append(
            jnp.concatenate([rows[:, 128 * b : 128 * b + 128] for b in range(8)], axis=0).T
        )
    return jnp.concatenate(turned, axis=0)


def column(gain_ref):
    row = lax.broadcasted_iota(jnp.int32, (HEAD_DIM, HEAD_DIM), 0)
    col = lax.broadcasted_iota(jnp.int32, (HEAD_DIM, HEAD_DIM), 1)
    spread = jnp.where(row == col, gain_ref[...], 0.0)
    return jnp.sum(spread, axis=1, keepdims=True)


def normed(values, gain):
    floats = values.astype(F32).reshape(HEADS, HEAD_DIM, TOKENS)
    inverse = lax.rsqrt(jnp.mean(floats * floats, axis=1, keepdims=True) + EPS)
    unit = floats * inverse
    return unit, inverse, (unit * gain[None]).astype(BF)


def normed_back(cotangent, unit, inverse, gain):
    scaled = cotangent * gain[None]
    along = jnp.mean(scaled * unit, axis=1, keepdims=True)
    grad = inverse * (scaled - unit * along)
    return grad.reshape(INNER, TOKENS).astype(BF), jnp.sum(cotangent * unit, axis=0)


def probabilities(query, key_in, same):
    weights = jnp.exp(dot(key_in, query, 0, 0) * SCALE)
    if same is not None:
        weights = weights * same
    return weights * (1.0 / jnp.sum(weights, axis=0, keepdims=True))


def scores_back(probs, query, key_in, value, cotangent):
    grad_probs = dot(value, cotangent, 0, 0)
    along = jnp.sum(probs * grad_probs, axis=0, keepdims=True)
    grad_scores = (probs * (grad_probs - along) * SCALE).astype(BF)
    grad_query = dot(key_in, grad_scores, 1, 0)
    grad_key = dot(query, grad_scores, 1, 1)
    return grad_query, grad_key


def head(values, index):
    return values[HEAD_DIM * index : HEAD_DIM * (index + 1), :]


def by_head(parts):
    return jnp.stack([part.astype(BF).astype(F32) for part in parts])


def load(sources, buffers, sems):
    copies = [
        pltpu.make_async_copy(source, buffer, sems.at[i])
        for i, (source, buffer) in enumerate(zip(sources, buffers))
    ]
    for copy in copies:
        copy.start()
    return copies


def send_kernel(*refs):
    sources, (out_ref, *buffers, sems) = refs[:9], refs[9:]
    copies = load(sources, buffers, sems)
    gain_q, gain_k, sq, sk, sv, tq, tk, og, tv_in = buffers
    for copy in copies[:4]:
        copy.wait()
    _, _, query = normed(sq[...], column(gain_q))
    _, _, key_in = normed(sk[...], column(gain_k))
    for copy in copies[4:]:
        copy.wait()
    value = sv[...]
    mixed = []
    for h in range(HEADS):
        probs = probabilities(query[h], key_in[h], None).astype(BF)
        mixed.append(dot(head(value, h), probs, 1, 0))
    spatial = jnp.concatenate(mixed, axis=0).astype(BF)
    total = (tv_in[...].astype(F32) + spatial.astype(F32)).astype(BF)
    pack(jnp.concatenate([tq[...], tk[...], og[...], total], axis=0), 18, out_ref)


def same_video(ids):
    ids = jnp.broadcast_to(ids.astype(F32), (TOKENS, TOKENS))
    return (ids == ids.T).astype(F32)


def temporal_first_kernel(in_ref, ids_hbm, gain_q_hbm, gain_k_hbm, out_ref, arrays_ref, ids, gain_q, gain_k, sems):
    copies = load((ids_hbm, gain_q_hbm, gain_k_hbm), (ids, gain_q, gain_k), sems)
    arrays = unpack(in_ref, 18)
    arrays_ref[...] = arrays
    for copy in copies:
        copy.wait()
    tq, tk, og = (arrays[INNER * i : INNER * (i + 1), :] for i in range(3))
    _, _, query = normed(tq, column(gain_q))
    _, _, key_in = normed(tk, column(gain_k))
    same = same_video(ids[...])
    grads_v = []
    for h in range(HEADS):
        probs = probabilities(query[h], key_in[h], same).astype(BF)
        grads_v.append(dot(head(og, h), probs, 1, 1))
    grad_v = jnp.concatenate(grads_v, axis=0).astype(BF)
    pack(jnp.concatenate([grad_v, jnp.zeros((192, TOKENS), BF)], axis=0), 6, out_ref)


def temporal_second_kernel(arrays_ref, ids_ref, gain_q, gain_k, out_ref, terms_ref):
    tq, tk, og, tv = (arrays_ref[INNER * i : INNER * (i + 1), :] for i in range(4))
    column_q, column_k = column(gain_q), column(gain_k)
    unit_q, inverse_q, query = normed(tq, column_q)
    unit_k, inverse_k, key_in = normed(tk, column_k)
    same = same_video(ids_ref[...])
    mixed, grads_q, grads_k = [], [], []
    for h in range(HEADS):
        probs = probabilities(query[h], key_in[h], same)
        value, cotangent = head(tv, h), head(og, h)
        mixed.append(dot(value, probs.astype(BF), 1, 0))
        grad_q, grad_k = scores_back(probs, query[h], key_in[h], value, cotangent)
        grads_q.append(grad_q)
        grads_k.append(grad_k)
    out = jnp.concatenate(mixed, axis=0).astype(BF)
    grad_q, terms_ref[0] = normed_back(by_head(grads_q), unit_q, inverse_q, column_q)
    grad_k, terms_ref[1] = normed_back(by_head(grads_k), unit_k, inverse_k, column_k)
    spare = jnp.zeros((320, TOKENS), BF)
    pack(jnp.concatenate([out, grad_q, grad_k, spare], axis=0), 16, out_ref)


def gain_rows(spatial, temporal):
    both = [jnp.sum(terms, axis=1, keepdims=True) for terms in (spatial, temporal)]
    high = [total.astype(BF).astype(F32) for total in both]
    low = [total - part for total, part in zip(both, high)]
    tiles = [
        [jnp.zeros((64, 1), F32), low[0][56:], low[1][56:], jnp.zeros((32, 1), F32)],
        [high[0], low[0][:56]],
        [high[1], low[1][:56]],
    ]
    row = lax.broadcasted_iota(jnp.int32, (16, 128), 0)
    rows = jnp.zeros((16, 128), F32)
    for i, parts in enumerate(tiles):
        tile = jnp.broadcast_to(jnp.concatenate(parts, axis=0), (128, 128)).T[:16, :]
        rows = rows + jnp.where(row == 13 + i, tile, 0.0)
    return rows


def spatial_back_kernel(
    in_ref, message, terms_ref, sq, sk, sv, gain_q, gain_k, out_ref, grad_tv, grad_sq, grad_sk, grad_sv
):
    given = unpack(in_ref, 6)[:INNER, :]
    grad_tv[...] = given
    column_q, column_k = column(gain_q), column(gain_k)
    unit_q, inverse_q, query = normed(sq[...], column_q)
    unit_k, inverse_k, key_in = normed(sk[...], column_k)
    value_all = sv[...]
    grads_q, grads_k, grads_v = [], [], []
    for h in range(HEADS):
        probs = probabilities(query[h], key_in[h], None)
        cotangent = head(given, h)
        grad_q, grad_k = scores_back(probs, query[h], key_in[h], head(value_all, h), cotangent)
        grads_q.append(grad_q)
        grads_k.append(grad_k)
        grads_v.append(dot(cotangent, probs.astype(BF), 1, 1))
    grad_sv[...] = jnp.concatenate(grads_v, axis=0).astype(BF)
    grad_sq[...], terms_q = normed_back(by_head(grads_q), unit_q, inverse_q, column_q)
    grad_sk[...], terms_k = normed_back(by_head(grads_k), unit_k, inverse_k, column_k)
    rows = jnp.stack([gain_rows(terms_q, terms_ref[0]), gain_rows(terms_k, terms_ref[1])])
    filled = message[...].astype(F32).reshape(64, 2, 16, 128) + rows[None]
    out_ref[...] = filled.astype(BF).reshape(2048, 128)


def gain_middle_kernel(in_ref, out_ref):
    total = jnp.sum(in_ref[...].astype(F32).reshape(128, 16, 128), axis=0)
    rest, spatial, temporal = (total[i : i + 1, :] for i in (13, 14, 15))
    pad = jnp.zeros((1, 128 - HEAD_DIM), F32)
    low = [
        jnp.concatenate([spatial[:, 72:], rest[:, 64:80], pad], axis=1),
        jnp.concatenate([temporal[:, 72:], rest[:, 80:96], pad], axis=1),
    ]
    rows = jnp.concatenate([spatial + low[0], temporal + low[1]], axis=0)
    out_ref[...] = jnp.broadcast_to(rows[None], out_ref.shape)


def last_kernel(in_ref, out, grad_tq, grad_tk):
    arrays = unpack(in_ref, 16)
    out[...], grad_tq[...], grad_tk[...] = (
        arrays[INNER * i : INNER * (i + 1), :] for i in range(3)
    )


def gain_last_kernel(in_ref, *outs):
    total = jnp.sum(in_ref[...].reshape(4, 2, 2, 128), axis=0)
    for i, out in enumerate(outs):
        out[...] = total[i % 2, i // 2 : i // 2 + 1, :HEAD_DIM]


def shape(*extent, dtype=BF):
    return jax.ShapeDtypeStruct(extent, dtype)


def call(kernel, out_shape, *args, in_hbm=0, scratch=(), work=0, vmem=32):
    specs = [pl.BlockSpec(memory_space=pltpu.VMEM)] * (len(args) - in_hbm)
    specs += [pl.BlockSpec(memory_space=pltpu.HBM)] * in_hbm
    split = len(args) - in_hbm
    args = args[:split] + tuple(
        pltpu.with_memory_space_constraint(a, pltpu.HBM) for a in args[split:]
    )
    cost = pl.CostEstimate(flops=work, bytes_accessed=0, transcendentals=0) if work else None
    return pl.pallas_call(
        kernel,
        out_shape=out_shape,
        in_specs=specs,
        scratch_shapes=scratch,
        compiler_params=pltpu.CompilerParams(vmem_limit_bytes=vmem * MIB),
        cost_estimate=cost,
    )(*args)


def buffers(*arrays):
    return [pltpu.VMEM(a.shape, a.dtype) for a in arrays] + [pltpu.SemaphoreType.DMA((len(arrays),))]


def exchange(message, axes, tiles):
    parts = message.reshape(TOKENS, tiles // 2, 2, 128)
    parts = lax.all_to_all(parts, axes, split_axis=0, concat_axis=0, tiled=True)
    return parts.reshape(TOKENS * tiles, 128)


def shards(
    spatial_query,
    spatial_key,
    spatial_value,
    temporal_query,
    temporal_key,
    temporal_value_in,
    out_grad,
    video_ids,
    spatial_query_gain,
    spatial_key_gain,
    temporal_query_gain,
    temporal_key_gain,
):
    sq, sk, sv, tq, tk, tv_in, og = (
        a.reshape(TOKENS, INNER).T
        for a in (
            spatial_query,
            spatial_key,
            spatial_value,
            temporal_query,
            temporal_key,
            temporal_value_in,
            out_grad,
        )
    )
    sq_gain, sk_gain, tq_gain, tk_gain = (
        g.reshape(1, HEAD_DIM)
        for g in (spatial_query_gain, spatial_key_gain, temporal_query_gain, temporal_key_gain)
    )
    seq = ("z", "y", "core")
    array = shape(INNER, TOKENS)
    args = (sq_gain, sk_gain, sq, sk, sv, tq, tk, og, tv_in)
    sent = call(send_kernel, shape(2304, 128), *args, in_hbm=9, scratch=buffers(*args))
    arrived = exchange(sent, seq, 18)
    args = (video_ids, tq_gain, tk_gain)
    sent, arrays = call(
        temporal_first_kernel,
        (shape(768, 128), shape(2304, 128)),
        arrived,
        *args,
        in_hbm=3,
        scratch=buffers(*args),
    )
    arrived = exchange(sent, seq, 6)
    message, terms = call(
        temporal_second_kernel,
        (shape(2048, 128), shape(2, HEAD_DIM, TOKENS, dtype=F32)),
        arrays,
        *args,
        work=4_000_000_000,
    )
    sent, grad_tv, grad_sq, grad_sk, grad_sv = call(
        spatial_back_kernel,
        (shape(2048, 128),) + (array,) * 4,
        arrived,
        message,
        terms,
        sq,
        sk,
        sv,
        sq_gain,
        sk_gain,
    )
    arrived = exchange(sent, seq, 16)
    gains = call(gain_middle_kernel, shape(8, 2, 128, dtype=F32), arrived)
    gains = lax.all_to_all(gains, ("dp", "core"), split_axis=0, concat_axis=0, tiled=True)
    out, grad_tq, grad_tk = call(last_kernel, (array,) * 3, arrived, work=1_000_000_000)
    gains = call(gain_last_kernel, (shape(1, HEAD_DIM, dtype=F32),) * 4, gains)
    results = (out, grad_sq, grad_sk, grad_sv, grad_tq, grad_tk, grad_tv)
    return tuple(a.T.reshape(1, 1, TOKENS, INNER) for a in results) + tuple(
        g.reshape(HEAD_DIM) for g in gains
    )


def solution(mesh):
    fine = Mesh(mesh.devices.reshape(4, 16, 4, 2), ("dp", "z", "y", "core"))
    tokens = P("dp", ("z", "y", "core"), None, None)
    return jax.shard_map(
        shards,
        mesh=fine,
        in_specs=(tokens,) * 7 + (P("dp", None),) + (P(),) * 4,
        out_specs=(tokens,) * 7 + (P(),) * 4,
        check_vma=False,
    )
```

```python
import jax
import jax.numpy as jnp
from jax import lax
from jax.experimental import pallas as pl
from jax.experimental.pallas import tpu as pltpu
from jax.sharding import Mesh
from jax.sharding import PartitionSpec as P

HEADS = 8
HEAD_DIM = 72
INNER = 576
TOKENS = 128
SCALE = HEAD_DIM ** (-0.5)
EPS = 1e-06
BF = jnp.bfloat16
F32 = jnp.float32
MIB = 1024 * 1024


def dot(left, right, left_dim, right_dim):
    return lax.dot_general(
        left, right, (((left_dim,), (right_dim,)), ((), ())), preferred_element_type=F32
    )


def pack(features, tiles, out_ref):
    size = 16 * tiles
    row = lax.broadcasted_iota(jnp.int32, (size, size), 0)
    col = lax.broadcasted_iota(jnp.int32, (size, size), 1)
    order = (row == (col & 15) * tiles + (col >> 4)).astype(F32).astype(BF)
    stacked = []
    for tile in range(tiles):
        turned = features[128 * tile : 128 * tile + 128, :].T
        stacked.append(
            jnp.concatenate([turned[16 * b : 16 * b + 16, :] for b in range(8)], axis=1)
        )
    mixed = dot(order, jnp.concatenate(stacked, axis=0), 1, 0).astype(BF)
    for b in range(8):
        out_ref[size * b : size * b + size, :] = mixed[:, 128 * b : 128 * b + 128]


def unpack(in_ref, tiles, wanted=None):
    wanted = wanted or tiles
    size = 16 * tiles
    row = lax.broadcasted_iota(jnp.int32, (16 * wanted, size), 0)
    col = lax.broadcasted_iota(jnp.int32, (16 * wanted, size), 1)
    order = (col == (row & 15) * tiles + (row >> 4)).astype(F32).astype(BF)
    blocks = jnp.concatenate(
        [in_ref[size * b : size * b + size, :] for b in range(8)], axis=1
    )
    mixed = dot(order, blocks, 1, 0).astype(BF)
    turned = []
    for tile in range(wanted):
        rows = mixed[16 * tile : 16 * tile + 16, :]
        turned.append(
            jnp.concatenate([rows[:, 128 * b : 128 * b + 128] for b in range(8)], axis=0).T
        )
    return jnp.concatenate(turned, axis=0)


def column(gain_ref):
    row = lax.broadcasted_iota(jnp.int32, (HEAD_DIM, HEAD_DIM), 0)
    col = lax.broadcasted_iota(jnp.int32, (HEAD_DIM, HEAD_DIM), 1)
    spread = jnp.where(row == col, gain_ref[...], 0.0)
    return jnp.sum(spread, axis=1, keepdims=True)


def normed(values, gain):
    floats = values.astype(F32).reshape(HEADS, HEAD_DIM, TOKENS)
    inverse = lax.rsqrt(jnp.mean(floats * floats, axis=1, keepdims=True) + EPS)
    unit = floats * inverse
    return unit, inverse, (unit * gain[None]).astype(BF)


def normed_back(cotangent, unit, inverse, gain):
    scaled = cotangent * gain[None]
    along = jnp.mean(scaled * unit, axis=1, keepdims=True)
    return (inverse * (scaled - unit * along)).reshape(INNER, TOKENS).astype(BF)


def gain_terms(cotangent, unit):
    return jnp.sum(jnp.sum(cotangent * unit, axis=0), axis=1, keepdims=True)


def probabilities(query, key_in, same):
    weights = jnp.exp(dot(key_in, query, 0, 0) * SCALE)
    if same is not None:
        weights = weights * same
    return weights * (1.0 / jnp.sum(weights, axis=0, keepdims=True))


def scores_back(probs, value, cotangent):
    grad_probs = dot(value, cotangent, 0, 0)
    along = jnp.sum(probs * grad_probs, axis=0, keepdims=True)
    return (probs * (grad_probs - along) * SCALE).astype(BF)


def head(values, index):
    return values[HEAD_DIM * index : HEAD_DIM * (index + 1), :]


def by_head(parts):
    return jnp.stack([part.astype(BF).astype(F32) for part in parts])


def load(sources, buffers, sems):
    copies = [
        pltpu.make_async_copy(source, buffer, sems.at[i])
        for i, (source, buffer) in enumerate(zip(sources, buffers))
    ]
    for copy in copies:
        copy.start()
    return copies


def send_kernel(*refs):
    sources, (out_ref, *buffers, sems) = refs[:9], refs[9:]
    copies = load(sources, buffers, sems)
    gain_q, gain_k, sq, sk, sv, tq, tk, og, tv_in = buffers
    for copy in copies[:4]:
        copy.wait()
    _, _, query = normed(sq[...], column(gain_q))
    _, _, key_in = normed(sk[...], column(gain_k))
    for copy in copies[4:]:
        copy.wait()
    value = sv[...]
    mixed = []
    for h in range(HEADS):
        probs = probabilities(query[h], key_in[h], None).astype(BF)
        mixed.append(dot(head(value, h), probs, 1, 0))
    spatial = jnp.concatenate(mixed, axis=0).astype(BF)
    total = (tv_in[...].astype(F32) + spatial.astype(F32)).astype(BF)
    pack(jnp.concatenate([tq[...], tk[...], og[...], total], axis=0), 18, out_ref)


def same_video(ids):
    ids = jnp.broadcast_to(ids.astype(F32), (TOKENS, TOKENS))
    return (ids == ids.T).astype(F32)


def temporal_kernel(in_ref, ids_hbm, gain_q_hbm, gain_k_hbm, out_ref, gains_ref, ids, gain_q, gain_k, sems):
    copies = load((ids_hbm, gain_q_hbm, gain_k_hbm), (ids, gain_q, gain_k), sems)
    arrays = unpack(in_ref, 18)
    tq, tk, og, tv = (arrays[INNER * i : INNER * (i + 1), :] for i in range(4))
    for copy in copies:
        copy.wait()
    column_q, column_k = column(gain_q), column(gain_k)
    unit_q, inverse_q, query = normed(tq, column_q)
    unit_k, inverse_k, key_in = normed(tk, column_k)
    same = same_video(ids[...])
    mixed, grads_q, grads_k, grads_v = [], [], [], []
    for h in range(HEADS):
        probs = probabilities(query[h], key_in[h], same)
        rounded = probs.astype(BF)
        value, cotangent = head(tv, h), head(og, h)
        mixed.append(dot(value, rounded, 1, 0))
        grads_v.append(dot(cotangent, rounded, 1, 1))
        scores = scores_back(probs, value, cotangent)
        grads_q.append(dot(key_in[h], scores, 1, 0))
        grads_k.append(dot(query[h], scores, 1, 1))
    out = jnp.concatenate(mixed, axis=0).astype(BF)
    grad_v = jnp.concatenate(grads_v, axis=0).astype(BF)
    grads_q, grads_k = by_head(grads_q), by_head(grads_k)
    gains_ref[...] = gain_terms(grads_q, unit_q)
    grad_q = normed_back(grads_q, unit_q, inverse_q, column_q)
    grad_k = normed_back(grads_k, unit_k, inverse_k, column_k)
    pack(jnp.concatenate([grad_v, out, grad_q, grad_k], axis=0), 18, out_ref)


def spatial_again_kernel(sq, sk, gain_q, gain_k, unit_q, unit_k, inverse_q, inverse_k, query, key_in, probs):
    unit_q[...], inverse_q[...], query[...] = normed(sq[...], column(gain_q))
    unit_k[...], inverse_k[...], key_in[...] = normed(sk[...], column(gain_k))
    for h in range(HEADS):
        probs[h] = probabilities(query[h], key_in[h], None)


def spatial_gain_kernel(in_ref, sv, unit_q, key_in, probs, temporal, grads_q, scores, out_ref):
    given = unpack(in_ref, 18, 5)
    for h in range(HEADS):
        scores[h] = scores_back(probs[h], head(sv, h), head(given, h))
        grads_q[h] = dot(key_in[h], scores[h], 1, 0).astype(BF)
    total = gain_terms(grads_q[...].astype(F32), unit_q[...])
    both = jnp.concatenate(
        [jnp.broadcast_to(t, (HEAD_DIM, 128)) for t in (total, temporal[...])], axis=0
    )
    both = jnp.concatenate([both, jnp.zeros((112, 128), F32)], axis=0)
    first, second = both[:128, :].T[:1, :], both[128:, :].T[:1, :]
    rows = jnp.concatenate([first, second], axis=0)
    out_ref[...] = jnp.broadcast_to(rows[None], out_ref.shape)


def spatial_rest_kernel(
    in_ref, unit_q, unit_k, inverse_q, inverse_k, query, probs, grads_q, scores, gain_q, gain_k,
    out, grad_tq, grad_tk, grad_tv, grad_sq, grad_sk, grad_sv
):
    arrays = unpack(in_ref, 18)
    grad_tv[...], out[...], grad_tq[...], grad_tk[...] = (
        arrays[INNER * i : INNER * (i + 1), :] for i in range(4)
    )
    grads_k, grads_v = [], []
    for h in range(HEADS):
        grads_k.append(dot(query[h], scores[h], 1, 1))
        grads_v.append(dot(head(arrays, h), probs[h].astype(BF), 1, 1))
    grad_sv[...] = jnp.concatenate(grads_v, axis=0).astype(BF)
    grad_sq[...] = normed_back(
        grads_q[...].astype(F32), unit_q[...], inverse_q[...], column(gain_q)
    )
    grad_sk[...] = normed_back(by_head(grads_k), unit_k[...], inverse_k[...], column(gain_k))


def gain_middle_kernel(in_ref, out_ref):
    out_ref[...] = jnp.broadcast_to(jnp.sum(in_ref[...], axis=0, keepdims=True), out_ref.shape)


def gain_last_kernel(in_ref, sq_gain, sk_gain, tq_gain, tk_gain, grad_sq, grad_sk, grad_tq, grad_tk):
    total = jnp.sum(in_ref[...], axis=0)
    spatial = total[:1, :HEAD_DIM]
    temporal = jnp.concatenate([total[:1, HEAD_DIM:], total[1:, : 2 * HEAD_DIM - 128]], axis=1)
    grad_sq[...] = spatial
    grad_sk[...] = spatial * (sq_gain[...] / sk_gain[...])
    grad_tq[...] = temporal
    grad_tk[...] = temporal * (tq_gain[...] / tk_gain[...])


def shape(*extent, dtype=BF):
    return jax.ShapeDtypeStruct(extent, dtype)


def call(kernel, out_shape, *args, in_hbm=0, scratch=(), work=0, vmem=32):
    specs = [pl.BlockSpec(memory_space=pltpu.VMEM)] * (len(args) - in_hbm)
    specs += [pl.BlockSpec(memory_space=pltpu.HBM)] * in_hbm
    split = len(args) - in_hbm
    args = args[:split] + tuple(
        pltpu.with_memory_space_constraint(a, pltpu.HBM) for a in args[split:]
    )
    cost = pl.CostEstimate(flops=work, bytes_accessed=0, transcendentals=0) if work else None
    return pl.pallas_call(
        kernel,
        out_shape=out_shape,
        in_specs=specs,
        scratch_shapes=scratch,
        compiler_params=pltpu.CompilerParams(vmem_limit_bytes=vmem * MIB),
        cost_estimate=cost,
    )(*args)


def buffers(*arrays):
    return [pltpu.VMEM(a.shape, a.dtype) for a in arrays] + [pltpu.SemaphoreType.DMA((len(arrays),))]


def exchange(message, axes, tiles):
    parts = message.reshape(TOKENS, tiles // 2, 2, 128)
    parts = lax.all_to_all(parts, axes, split_axis=0, concat_axis=0, tiled=True)
    return parts.reshape(TOKENS * tiles, 128)


def shards(
    spatial_query,
    spatial_key,
    spatial_value,
    temporal_query,
    temporal_key,
    temporal_value_in,
    out_grad,
    video_ids,
    spatial_query_gain,
    spatial_key_gain,
    temporal_query_gain,
    temporal_key_gain,
):
    sq, sk, sv, tq, tk, tv_in, og = (
        a.reshape(TOKENS, INNER).T
        for a in (
            spatial_query,
            spatial_key,
            spatial_value,
            temporal_query,
            temporal_key,
            temporal_value_in,
            out_grad,
        )
    )
    sq_gain, sk_gain, tq_gain, tk_gain = (
        g.reshape(1, HEAD_DIM)
        for g in (spatial_query_gain, spatial_key_gain, temporal_query_gain, temporal_key_gain)
    )
    seq = ("z", "y", "core")
    array = shape(INNER, TOKENS)
    args = (sq_gain, sk_gain, sq, sk, sv, tq, tk, og, tv_in)
    sent = call(send_kernel, shape(2304, 128), *args, in_hbm=9, scratch=buffers(*args))
    arrived = exchange(sent, seq, 18)
    args = (video_ids, tq_gain, tk_gain)
    sent, temporal = call(
        temporal_kernel,
        (shape(2304, 128), shape(HEAD_DIM, 1, dtype=F32)),
        arrived,
        *args,
        in_hbm=3,
        scratch=buffers(*args),
    )
    arrived = exchange(sent, seq, 18)
    unit, inverse = shape(HEADS, HEAD_DIM, TOKENS, dtype=F32), shape(HEADS, 1, TOKENS, dtype=F32)
    normal = shape(HEADS, HEAD_DIM, TOKENS)
    unit_q, unit_k, inverse_q, inverse_k, query, key_in, probs = call(
        spatial_again_kernel,
        (unit, unit, inverse, inverse, normal, normal, shape(HEADS, 128, 128, dtype=F32)),
        sq,
        sk,
        sq_gain,
        sk_gain,
        work=2_000_000_000,
    )
    grads_q, scores, gains = call(
        spatial_gain_kernel,
        (normal, shape(HEADS, 128, 128), shape(16, 2, 128, dtype=F32)),
        arrived,
        sv,
        unit_q,
        key_in,
        probs,
        temporal,
    )
    gains = lax.all_to_all(gains, "z", split_axis=0, concat_axis=0, tiled=True)
    out, grad_tq, grad_tk, grad_tv, grad_sq, grad_sk, grad_sv = call(
        spatial_rest_kernel,
        (array,) * 7,
        arrived,
        unit_q,
        unit_k,
        inverse_q,
        inverse_k,
        query,
        probs,
        grads_q,
        scores,
        sq_gain,
        sk_gain,
        work=3_000_000_000,
    )
    gains = call(gain_middle_kernel, shape(32, 2, 128, dtype=F32), gains)
    gains = lax.all_to_all(gains, ("core", "y", "dp"), split_axis=0, concat_axis=0, tiled=True)
    gains = call(
        gain_last_kernel,
        (shape(1, HEAD_DIM, dtype=F32),) * 4,
        gains,
        sq_gain,
        sk_gain,
        tq_gain,
        tk_gain,
    )
    results = (out, grad_sq, grad_sk, grad_sv, grad_tq, grad_tk, grad_tv)
    return tuple(a.T.reshape(1, 1, TOKENS, INNER) for a in results) + tuple(
        g.reshape(HEAD_DIM) for g in gains
    )


def solution(mesh):
    fine = Mesh(mesh.devices.reshape(4, 16, 4, 2), ("dp", "z", "y", "core"))
    tokens = P("dp", ("z", "y", "core"), None, None)
    return jax.shard_map(
        shards,
        mesh=fine,
        in_specs=(tokens,) * 7 + (P("dp", None),) + (P(),) * 4,
        out_specs=(tokens,) * 7 + (P(),) * 4,
        check_vma=False,
    )
```

```python
import jax
import jax.numpy as jnp
from jax import lax
from jax.experimental import pallas as pl
from jax.experimental.pallas import tpu as pltpu
from jax.sharding import Mesh
from jax.sharding import PartitionSpec as P

HEADS = 8
HEAD_DIM = 72
INNER = 576
TOKENS = 128
SCALE = HEAD_DIM ** (-0.5)
EPS = 1e-06
EARLY = 192
BF = jnp.bfloat16
F32 = jnp.float32
MIB = 1024 * 1024


def dot(left, right, left_dim, right_dim):
    return lax.dot_general(
        left, right, (((left_dim,), (right_dim,)), ((), ())), preferred_element_type=F32
    )


def pack(features, tiles, out_ref):
    size = 16 * tiles
    row = lax.broadcasted_iota(jnp.int32, (size, size), 0)
    col = lax.broadcasted_iota(jnp.int32, (size, size), 1)
    order = (row == (col & 15) * tiles + (col >> 4)).astype(F32).astype(BF)
    stacked = []
    for tile in range(tiles):
        turned = features[128 * tile : 128 * tile + 128, :].T
        stacked.append(
            jnp.concatenate([turned[16 * b : 16 * b + 16, :] for b in range(8)], axis=1)
        )
    mixed = dot(order, jnp.concatenate(stacked, axis=0), 1, 0).astype(BF)
    for b in range(8):
        out_ref[size * b : size * b + size, :] = mixed[:, 128 * b : 128 * b + 128]


def token_tiles(in_ref, tiles, wanted):
    size = 16 * tiles
    row = lax.broadcasted_iota(jnp.int32, (16 * wanted, size), 0)
    col = lax.broadcasted_iota(jnp.int32, (16 * wanted, size), 1)
    order = (col == (row & 15) * tiles + (row >> 4)).astype(F32).astype(BF)
    blocks = jnp.concatenate(
        [in_ref[size * b : size * b + size, :] for b in range(8)], axis=1
    )
    mixed = dot(order, blocks, 1, 0).astype(BF)
    return [
        jnp.concatenate(
            [mixed[16 * tile : 16 * tile + 16, 128 * b : 128 * b + 128] for b in range(8)], axis=0
        )
        for tile in range(wanted)
    ]


def unpack(in_ref, tiles, wanted=None):
    return jnp.concatenate([t.T for t in token_tiles(in_ref, tiles, wanted or tiles)], axis=0)


def column(gain_ref):
    row = lax.broadcasted_iota(jnp.int32, (HEAD_DIM, HEAD_DIM), 0)
    col = lax.broadcasted_iota(jnp.int32, (HEAD_DIM, HEAD_DIM), 1)
    spread = jnp.where(row == col, gain_ref[...], 0.0)
    return jnp.sum(spread, axis=1, keepdims=True)


def normed(values, gain):
    floats = values.astype(F32).reshape(HEADS, HEAD_DIM, TOKENS)
    inverse = lax.rsqrt(jnp.mean(floats * floats, axis=1, keepdims=True) + EPS)
    unit = floats * inverse
    return unit, inverse, (unit * gain[None]).astype(BF)


def normed_back(cotangent, unit, inverse, gain):
    scaled = cotangent * gain[None]
    along = jnp.mean(scaled * unit, axis=1, keepdims=True)
    return (inverse * (scaled - unit * along)).reshape(INNER, TOKENS).astype(BF)


def gain_terms(cotangent, unit):
    return jnp.sum(jnp.sum(cotangent * unit, axis=0), axis=1, keepdims=True)


def probabilities(query, key_in, same):
    weights = jnp.exp(dot(key_in, query, 0, 0) * SCALE)
    if same is not None:
        weights = weights * same
    return weights * (1.0 / jnp.sum(weights, axis=0, keepdims=True))


def scores_back(probs, value, cotangent):
    grad_probs = dot(value, cotangent, 0, 0)
    along = jnp.sum(probs * grad_probs, axis=0, keepdims=True)
    return (probs * (grad_probs - along) * SCALE).astype(BF)


def head(values, index):
    return values[HEAD_DIM * index : HEAD_DIM * (index + 1), :]


def by_head(parts):
    return jnp.stack([part.astype(BF).astype(F32) for part in parts])


def load(sources, buffers, sems):
    copies = [
        pltpu.make_async_copy(source, buffer, sems.at[i])
        for i, (source, buffer) in enumerate(zip(sources, buffers))
    ]
    for copy in copies:
        copy.start()
    return copies


def send_kernel(*refs):
    sources, (out_ref, unit_q, unit_k, inverse_q, inverse_k, query, key_in, probs) = refs[:9], refs[9:17]
    buffers, sems = refs[17:-1], refs[-1]
    copies = load(sources, buffers, sems)
    gain_q, gain_k, sq, sk, sv, tq, tk, og, tv_in = buffers
    for copy in copies[:4]:
        copy.wait()
    unit_q[...], inverse_q[...], query[...] = normed(sq[...], column(gain_q))
    unit_k[...], inverse_k[...], key_in[...] = normed(sk[...], column(gain_k))
    for copy in copies[4:]:
        copy.wait()
    mixed = []
    for h in range(HEADS):
        probs[h] = probabilities(query[h], key_in[h], None)
        mixed.append(dot(head(sv, h), probs[h].astype(BF), 1, 0))
    spatial = jnp.concatenate(mixed, axis=0).astype(BF)
    total = (tv_in[...].astype(F32) + spatial.astype(F32)).astype(BF)
    pack(jnp.concatenate([tq[...], tk[...], og[...], total], axis=0), 18, out_ref)


def same_video(ids):
    ids = jnp.broadcast_to(ids.astype(F32), (TOKENS, TOKENS))
    return (ids == ids.T).astype(F32)


def temporal_kernel(
    in_ref, ids_hbm, gain_q_hbm, gain_k_hbm, out_ref, later_ref, gains_ref, ids, gain_q, gain_k, sems
):
    copies = load((ids_hbm, gain_q_hbm, gain_k_hbm), (ids, gain_q, gain_k), sems)
    arrays = unpack(in_ref, 18)
    tq, tk, og, tv = (arrays[INNER * i : INNER * (i + 1), :] for i in range(4))
    for copy in copies:
        copy.wait()
    column_q, column_k = column(gain_q), column(gain_k)
    unit_q, inverse_q, query = normed(tq, column_q)
    unit_k, inverse_k, key_in = normed(tk, column_k)
    same = same_video(ids[...])
    mixed, grads_q, grads_k, grads_v = [], [], [], []
    for h in range(HEADS):
        probs = probabilities(query[h], key_in[h], same)
        rounded = probs.astype(BF)
        value, cotangent = head(tv, h), head(og, h)
        mixed.append(dot(value, rounded, 1, 0))
        grads_v.append(dot(cotangent, rounded, 1, 1))
        scores = scores_back(probs, value, cotangent)
        grads_q.append(dot(key_in[h], scores, 1, 0))
        grads_k.append(dot(query[h], scores, 1, 1))
    out = jnp.concatenate(mixed, axis=0).astype(BF)
    grad_v = jnp.concatenate(grads_v, axis=0).astype(BF)
    grads_q, grads_k = by_head(grads_q), by_head(grads_k)
    gains_ref[...] = gain_terms(grads_q, unit_q)
    grad_q = normed_back(grads_q, unit_q, inverse_q, column_q)
    grad_k = normed_back(grads_k, unit_k, inverse_k, column_k)
    later_ref[...] = jnp.concatenate([out[EARLY:, :], grad_q, grad_k], axis=0)
    pack(jnp.concatenate([grad_v, out[:EARLY, :]], axis=0), 6, out_ref)


def spatial_gain_kernel(in_ref, sv, unit_q, key_in, probs, temporal, grads_q, scores, out_ref):
    given = unpack(in_ref, 6, 5)
    for h in range(HEADS):
        scores[h] = scores_back(probs[h], head(sv, h), head(given, h))
        grads_q[h] = dot(key_in[h], scores[h], 1, 0).astype(BF)
    total = gain_terms(grads_q[...].astype(F32), unit_q[...])
    both = jnp.concatenate(
        [jnp.broadcast_to(t, (HEAD_DIM, 128)) for t in (total, temporal[...])], axis=0
    )
    both = jnp.concatenate([both, jnp.zeros((112, 128), F32)], axis=0)
    rows = jnp.concatenate([both[:128, :].T[:1, :], both[128:, :].T[:1, :]], axis=0)
    out_ref[...] = jnp.broadcast_to(rows[None], out_ref.shape)


def spatial_rest_kernel(
    in_ref, later, unit_q, unit_k, inverse_q, inverse_k, query, probs, grads_q, scores, gain_q, gain_k,
    message, out_early, grad_tv, grad_sq, grad_sk, grad_sv
):
    arrays = unpack(in_ref, 6)
    grad_tv[...], out_early[...] = arrays[:INNER, :], arrays[INNER:, :]
    grads_k, grads_v = [], []
    for h in range(HEADS):
        grads_k.append(dot(query[h], scores[h], 1, 1))
        grads_v.append(dot(head(arrays, h), probs[h].astype(BF), 1, 1))
    grad_sv[...] = jnp.concatenate(grads_v, axis=0).astype(BF)
    grad_sq[...] = normed_back(
        grads_q[...].astype(F32), unit_q[...], inverse_q[...], column(gain_q)
    )
    grad_sk[...] = normed_back(by_head(grads_k), unit_k[...], inverse_k[...], column(gain_k))
    pack(jnp.concatenate([later[...], jnp.zeros((256, TOKENS), BF)], axis=0), 14, message)


def fill_kernel(gains, message, out_ref):
    total = jnp.sum(gains[...], axis=0)
    high = total.astype(BF).astype(F32)
    part = jnp.where(lax.axis_index("core") == 0, high, total - high)
    row = lax.broadcasted_iota(jnp.int32, (224, 128), 0)
    place = row - 14 * ((row * 4682) >> 16)
    block = jnp.where(place == 12, part[:1, :], part[1:, :])
    for b in range(8):
        rows = message[224 * b : 224 * b + 224, :].astype(F32)
        out_ref[224 * b : 224 * b + 224, :] = jnp.where(place >= 12, block, rows).astype(BF)


def last_kernel(
    in_ref, out_early, sq_gain, sk_gain, tq_gain, tk_gain,
    out, grad_tq, grad_tk, grad_sq_gain, grad_sk_gain, grad_tq_gain, grad_tk_gain
):
    tiles = token_tiles(in_ref, 14, 14)
    first, second = (jnp.sum(t.astype(F32), axis=0, keepdims=True) for t in tiles[12:])
    spatial = first[:, :HEAD_DIM]
    temporal = jnp.concatenate([first[:, HEAD_DIM:], second[:, : 2 * HEAD_DIM - 128]], axis=1)
    grad_sq_gain[...] = spatial
    grad_sk_gain[...] = spatial * (sq_gain[...] / sk_gain[...])
    grad_tq_gain[...] = temporal
    grad_tk_gain[...] = temporal * (tq_gain[...] / tk_gain[...])
    arrays = jnp.concatenate([t.T for t in tiles[:12]], axis=0)
    rest = INNER - EARLY
    out[...] = jnp.concatenate([out_early[...], arrays[:rest, :]], axis=0)
    grad_tq[...] = arrays[rest : rest + INNER, :]
    grad_tk[...] = arrays[rest + INNER :, :]


def shape(*extent, dtype=BF):
    return jax.ShapeDtypeStruct(extent, dtype)


def call(kernel, out_shape, *args, in_hbm=0, scratch=(), work=0, vmem=32):
    specs = [pl.BlockSpec(memory_space=pltpu.VMEM)] * (len(args) - in_hbm)
    specs += [pl.BlockSpec(memory_space=pltpu.HBM)] * in_hbm
    split = len(args) - in_hbm
    args = args[:split] + tuple(
        pltpu.with_memory_space_constraint(a, pltpu.HBM) for a in args[split:]
    )
    cost = pl.CostEstimate(flops=work, bytes_accessed=0, transcendentals=0) if work else None
    return pl.pallas_call(
        kernel,
        out_shape=out_shape,
        in_specs=specs,
        scratch_shapes=scratch,
        compiler_params=pltpu.CompilerParams(vmem_limit_bytes=vmem * MIB),
        cost_estimate=cost,
    )(*args)


def buffers(*arrays):
    return [pltpu.VMEM(a.shape, a.dtype) for a in arrays] + [pltpu.SemaphoreType.DMA((len(arrays),))]


def exchange(message, axes, tiles):
    parts = message.reshape(TOKENS, tiles // 2, 2, 128)
    parts = lax.all_to_all(parts, axes, split_axis=0, concat_axis=0, tiled=True)
    return parts.reshape(TOKENS * tiles, 128)


def shards(
    spatial_query,
    spatial_key,
    spatial_value,
    temporal_query,
    temporal_key,
    temporal_value_in,
    out_grad,
    video_ids,
    spatial_query_gain,
    spatial_key_gain,
    temporal_query_gain,
    temporal_key_gain,
):
    sq, sk, sv, tq, tk, tv_in, og = (
        a.reshape(TOKENS, INNER).T
        for a in (
            spatial_query,
            spatial_key,
            spatial_value,
            temporal_query,
            temporal_key,
            temporal_value_in,
            out_grad,
        )
    )
    sq_gain, sk_gain, tq_gain, tk_gain = (
        g.reshape(1, HEAD_DIM)
        for g in (spatial_query_gain, spatial_key_gain, temporal_query_gain, temporal_key_gain)
    )
    seq = ("z", "y", "core")
    array = shape(INNER, TOKENS)
    args = (sq_gain, sk_gain, sq, sk, sv, tq, tk, og, tv_in)
    unit, inverse = shape(HEADS, HEAD_DIM, TOKENS, dtype=F32), shape(HEADS, 1, TOKENS, dtype=F32)
    normal, square = shape(HEADS, HEAD_DIM, TOKENS), shape(HEADS, 128, 128)
    sent, unit_q, unit_k, inverse_q, inverse_k, query, key_in, probs = call(
        send_kernel,
        (shape(2304, 128), unit, unit, inverse, inverse, normal, normal, shape(HEADS, 128, 128, dtype=F32)),
        *args,
        in_hbm=9,
        scratch=buffers(*args),
    )
    arrived = exchange(sent, seq, 18)
    args = (video_ids, tq_gain, tk_gain)
    sent, later, temporal = call(
        temporal_kernel,
        (shape(768, 128), shape(1536, 128), shape(HEAD_DIM, 1, dtype=F32)),
        arrived,
        *args,
        in_hbm=3,
        scratch=buffers(*args),
    )
    arrived = exchange(sent, seq, 6)
    grads_q, scores, gains = call(
        spatial_gain_kernel,
        (normal, square, shape(8, 2, 128, dtype=F32)),
        arrived,
        sv,
        unit_q,
        key_in,
        probs,
        temporal,
    )
    gains = lax.all_to_all(gains, ("dp", "core"), split_axis=0, concat_axis=0, tiled=True)
    message, out_early, grad_tv, grad_sq, grad_sk, grad_sv = call(
        spatial_rest_kernel,
        (shape(1792, 128), shape(EARLY, TOKENS)) + (array,) * 4,
        arrived,
        later,
        unit_q,
        unit_k,
        inverse_q,
        inverse_k,
        query,
        probs,
        grads_q,
        scores,
        sq_gain,
        sk_gain,
        work=3_000_000_000,
    )
    sent = call(fill_kernel, shape(1792, 128), gains, message)
    arrived = exchange(sent, seq, 14)
    gain = shape(1, HEAD_DIM, dtype=F32)
    out, grad_tq, grad_tk, *gains = call(
        last_kernel,
        (array,) * 3 + (gain,) * 4,
        arrived,
        out_early,
        sq_gain,
        sk_gain,
        tq_gain,
        tk_gain,
    )
    results = (out, grad_sq, grad_sk, grad_sv, grad_tq, grad_tk, grad_tv)
    return tuple(a.T.reshape(1, 1, TOKENS, INNER) for a in results) + tuple(
        g.reshape(HEAD_DIM) for g in gains
    )


def solution(mesh):
    fine = Mesh(mesh.devices.reshape(4, 16, 4, 2), ("dp", "z", "y", "core"))
    tokens = P("dp", ("z", "y", "core"), None, None)
    return jax.shard_map(
        shards,
        mesh=fine,
        in_specs=(tokens,) * 7 + (P("dp", None),) + (P(),) * 4,
        out_specs=(tokens,) * 7 + (P(),) * 4,
        check_vma=False,
    )
```

```python
import jax
import jax.numpy as jnp
from jax import lax
from jax.experimental import pallas as pl
from jax.experimental.pallas import tpu as pltpu
from jax.sharding import Mesh
from jax.sharding import PartitionSpec as P

HEADS = 8
HEAD_DIM = 72
INNER = 576
TOKENS = 128
SCALE = HEAD_DIM ** (-0.5)
EPS = 1e-06
EARLY = 192
BF = jnp.bfloat16
F32 = jnp.float32
MIB = 1024 * 1024


def dot(left, right, left_dim, right_dim):
    return lax.dot_general(
        left, right, (((left_dim,), (right_dim,)), ((), ())), preferred_element_type=F32
    )


def pack(features, tiles, out_ref):
    size = 16 * tiles
    row = lax.broadcasted_iota(jnp.int32, (size, size), 0)
    col = lax.broadcasted_iota(jnp.int32, (size, size), 1)
    order = (row == (col & 15) * tiles + (col >> 4)).astype(F32).astype(BF)
    stacked = []
    for tile in range(tiles):
        turned = features[128 * tile : 128 * tile + 128, :].T
        stacked.append(
            jnp.concatenate([turned[16 * b : 16 * b + 16, :] for b in range(8)], axis=1)
        )
    mixed = dot(order, jnp.concatenate(stacked, axis=0), 1, 0).astype(BF)
    for b in range(8):
        out_ref[size * b : size * b + size, :] = mixed[:, 128 * b : 128 * b + 128]


def token_tiles(in_ref, tiles, wanted):
    size = 16 * tiles
    row = lax.broadcasted_iota(jnp.int32, (16 * wanted, size), 0)
    col = lax.broadcasted_iota(jnp.int32, (16 * wanted, size), 1)
    order = (col == (row & 15) * tiles + (row >> 4)).astype(F32).astype(BF)
    blocks = jnp.concatenate(
        [in_ref[size * b : size * b + size, :] for b in range(8)], axis=1
    )
    mixed = dot(order, blocks, 1, 0).astype(BF)
    return [
        jnp.concatenate(
            [mixed[16 * tile : 16 * tile + 16, 128 * b : 128 * b + 128] for b in range(8)], axis=0
        )
        for tile in range(wanted)
    ]


def unpack(in_ref, tiles, wanted=None):
    return jnp.concatenate([t.T for t in token_tiles(in_ref, tiles, wanted or tiles)], axis=0)


def column(gain_ref):
    row = lax.broadcasted_iota(jnp.int32, (HEAD_DIM, HEAD_DIM), 0)
    col = lax.broadcasted_iota(jnp.int32, (HEAD_DIM, HEAD_DIM), 1)
    spread = jnp.where(row == col, gain_ref[...], 0.0)
    return jnp.sum(spread, axis=1, keepdims=True)


def normed(values, gain):
    floats = values.astype(F32).reshape(HEADS, HEAD_DIM, TOKENS)
    inverse = lax.rsqrt(jnp.mean(floats * floats, axis=1, keepdims=True) + EPS)
    unit = floats * inverse
    return unit, inverse, (unit * gain[None]).astype(BF)


def normed_back(cotangent, unit, inverse, gain):
    scaled = cotangent * gain[None]
    along = jnp.mean(scaled * unit, axis=1, keepdims=True)
    return (inverse * (scaled - unit * along)).reshape(INNER, TOKENS).astype(BF)


def gain_terms(cotangent, unit):
    return jnp.sum(jnp.sum(cotangent * unit, axis=0), axis=1, keepdims=True)


def probabilities(query, key_in, same):
    products = [dot(key_in[h], query[h], 0, 0) for h in range(HEADS)]
    weights = [jnp.exp(product * SCALE) for product in products]
    if same is not None:
        weights = [weight * same for weight in weights]
    return [weight * (1.0 / jnp.sum(weight, axis=0, keepdims=True)) for weight in weights]


def scores_back(probs, grad_probs):
    along = [jnp.sum(p * g, axis=0, keepdims=True) for p, g in zip(probs, grad_probs)]
    return [(p * (g - a) * SCALE).astype(BF) for p, g, a in zip(probs, grad_probs, along)]


def heads(values):
    return [values[HEAD_DIM * h : HEAD_DIM * (h + 1), :] for h in range(HEADS)]


def dots(left, right, left_dim, right_dim):
    return [dot(left[h], right[h], left_dim, right_dim) for h in range(HEADS)]


def by_head(parts):
    return jnp.stack([part.astype(BF).astype(F32) for part in parts])


def load(sources, buffers, sems):
    copies = [
        pltpu.make_async_copy(source, buffer, sems.at[i])
        for i, (source, buffer) in enumerate(zip(sources, buffers))
    ]
    for copy in copies:
        copy.start()
    return copies


def send_kernel(*refs):
    sources, (out_ref, unit_q, unit_k, inverse_q, inverse_k, query, key_in, probs) = refs[:9], refs[9:17]
    buffers, sems = refs[17:-1], refs[-1]
    copies = load(sources, buffers, sems)
    gain_q, gain_k, sq, sk, sv, tq, tk, og, tv_in = buffers
    for copy in copies[:4]:
        copy.wait()
    unit_q[...], inverse_q[...], query[...] = normed(sq[...], column(gain_q))
    unit_k[...], inverse_k[...], key_in[...] = normed(sk[...], column(gain_k))
    for copy in copies[4:]:
        copy.wait()
    found = probabilities(query, key_in, None)
    for h in range(HEADS):
        probs[h] = found[h]
    mixed = dots(heads(sv), [p.astype(BF) for p in found], 1, 0)
    spatial = jnp.concatenate(mixed, axis=0).astype(BF)
    total = (tv_in[...].astype(F32) + spatial.astype(F32)).astype(BF)
    pack(jnp.concatenate([tq[...], tk[...], og[...], total], axis=0), 18, out_ref)


def same_video(ids):
    ids = jnp.broadcast_to(ids.astype(F32), (TOKENS, TOKENS))
    return (ids == ids.T).astype(F32)


def temporal_kernel(
    in_ref, ids_hbm, gain_q_hbm, gain_k_hbm, out_ref, later_ref, gains_ref, ids, gain_q, gain_k, sems
):
    copies = load((ids_hbm, gain_q_hbm, gain_k_hbm), (ids, gain_q, gain_k), sems)
    arrays = unpack(in_ref, 18)
    tq, tk, og, tv = (arrays[INNER * i : INNER * (i + 1), :] for i in range(4))
    for copy in copies:
        copy.wait()
    column_q, column_k = column(gain_q), column(gain_k)
    unit_q, inverse_q, query = normed(tq, column_q)
    unit_k, inverse_k, key_in = normed(tk, column_k)
    same = same_video(ids[...])
    values, cotangents = heads(tv), heads(og)
    probs = probabilities(query, key_in, same)
    grad_probs = dots(values, cotangents, 0, 0)
    rounded = [p.astype(BF) for p in probs]
    out = jnp.concatenate(dots(values, rounded, 1, 0), axis=0).astype(BF)
    grad_v = jnp.concatenate(dots(cotangents, rounded, 1, 1), axis=0).astype(BF)
    scores = scores_back(probs, grad_probs)
    grads_q = by_head(dots(key_in, scores, 1, 0))
    grads_k = by_head(dots(query, scores, 1, 1))
    gains_ref[...] = gain_terms(grads_q, unit_q)
    grad_q = normed_back(grads_q, unit_q, inverse_q, column_q)
    grad_k = normed_back(grads_k, unit_k, inverse_k, column_k)
    later_ref[...] = jnp.concatenate([out[EARLY:, :], grad_q, grad_k], axis=0)
    pack(jnp.concatenate([grad_v, out[:EARLY, :]], axis=0), 6, out_ref)


def spatial_gain_kernel(in_ref, sv, unit_q, key_in, probs, temporal, grads_q, scores, out_ref):
    given = unpack(in_ref, 6, 5)
    found = scores_back([probs[h] for h in range(HEADS)], dots(heads(sv), heads(given), 0, 0))
    products = [p.astype(BF) for p in dots(key_in, found, 1, 0)]
    for h in range(HEADS):
        scores[h] = found[h]
        grads_q[h] = products[h]
    total = gain_terms(by_head(products), unit_q[...])
    both = jnp.concatenate(
        [jnp.broadcast_to(t, (HEAD_DIM, 128)) for t in (total, temporal[...])], axis=0
    )
    both = jnp.concatenate([both, jnp.zeros((112, 128), F32)], axis=0)
    rows = jnp.concatenate([both[:128, :].T[:1, :], both[128:, :].T[:1, :]], axis=0)
    out_ref[...] = jnp.broadcast_to(rows[None], out_ref.shape)


def spatial_rest_kernel(
    in_ref, later, unit_q, unit_k, inverse_q, inverse_k, query, probs, grads_q, scores, gain_q, gain_k, gain_tq, gain_tk,
    ratios, message, out_early, grad_tv, grad_sq, grad_sk, grad_sv
):
    ratios[...] = jnp.concatenate([gain_q[...] / gain_k[...], gain_tq[...] / gain_tk[...]], axis=0)
    arrays = unpack(in_ref, 6)
    grad_tv[...], out_early[...] = arrays[:INNER, :], arrays[INNER:, :]
    grads_k = dots(query, scores, 1, 1)
    grads_v = dots(heads(arrays), [probs[h].astype(BF) for h in range(HEADS)], 1, 1)
    grad_sv[...] = jnp.concatenate(grads_v, axis=0).astype(BF)
    grad_sq[...] = normed_back(
        grads_q[...].astype(F32), unit_q[...], inverse_q[...], column(gain_q)
    )
    grad_sk[...] = normed_back(by_head(grads_k), unit_k[...], inverse_k[...], column(gain_k))
    pack(jnp.concatenate([later[...], jnp.zeros((256, TOKENS), BF)], axis=0), 14, message)


def fill_kernel(gains, message, out_ref):
    total = jnp.sum(gains[...], axis=0)
    high = total.astype(BF).astype(F32)
    part = jnp.where(lax.axis_index("core") == 0, high, total - high)
    row = lax.broadcasted_iota(jnp.int32, (224, 128), 0)
    place = row - 14 * ((row * 4682) >> 16)
    block = jnp.where(place == 12, part[:1, :], part[1:, :])
    for b in range(8):
        rows = message[224 * b : 224 * b + 224, :].astype(F32)
        out_ref[224 * b : 224 * b + 224, :] = jnp.where(place >= 12, block, rows).astype(BF)


def last_kernel(
    in_ref, out_early, ratios,
    out, grad_tq, grad_tk, grad_sq_gain, grad_sk_gain, grad_tq_gain, grad_tk_gain
):
    tiles = token_tiles(in_ref, 14, 14)
    first, second = (jnp.sum(t.astype(F32), axis=0, keepdims=True) for t in tiles[12:])
    spatial = first[:, :HEAD_DIM]
    temporal = jnp.concatenate([first[:, HEAD_DIM:], second[:, : 2 * HEAD_DIM - 128]], axis=1)
    grad_sq_gain[...] = spatial
    grad_sk_gain[...] = spatial * ratios[:1, :]
    grad_tq_gain[...] = temporal
    grad_tk_gain[...] = temporal * ratios[1:, :]
    arrays = jnp.concatenate([t.T for t in tiles[:12]], axis=0)
    rest = INNER - EARLY
    out[...] = jnp.concatenate([out_early[...], arrays[:rest, :]], axis=0)
    grad_tq[...] = arrays[rest : rest + INNER, :]
    grad_tk[...] = arrays[rest + INNER :, :]


def shape(*extent, dtype=BF):
    return jax.ShapeDtypeStruct(extent, dtype)


def call(kernel, out_shape, *args, in_hbm=0, scratch=(), work=0, vmem=32):
    specs = [pl.BlockSpec(memory_space=pltpu.VMEM)] * (len(args) - in_hbm)
    specs += [pl.BlockSpec(memory_space=pltpu.HBM)] * in_hbm
    split = len(args) - in_hbm
    args = args[:split] + tuple(
        pltpu.with_memory_space_constraint(a, pltpu.HBM) for a in args[split:]
    )
    cost = pl.CostEstimate(flops=work, bytes_accessed=0, transcendentals=0) if work else None
    return pl.pallas_call(
        kernel,
        out_shape=out_shape,
        in_specs=specs,
        scratch_shapes=scratch,
        compiler_params=pltpu.CompilerParams(vmem_limit_bytes=vmem * MIB),
        cost_estimate=cost,
    )(*args)


def buffers(*arrays):
    return [pltpu.VMEM(a.shape, a.dtype) for a in arrays] + [pltpu.SemaphoreType.DMA((len(arrays),))]


def exchange(message, axes, tiles):
    parts = message.reshape(TOKENS, tiles // 2, 2, 128)
    parts = lax.all_to_all(parts, axes, split_axis=0, concat_axis=0, tiled=True)
    return parts.reshape(TOKENS * tiles, 128)


def shards(
    spatial_query,
    spatial_key,
    spatial_value,
    temporal_query,
    temporal_key,
    temporal_value_in,
    out_grad,
    video_ids,
    spatial_query_gain,
    spatial_key_gain,
    temporal_query_gain,
    temporal_key_gain,
):
    sq, sk, sv, tq, tk, tv_in, og = (
        a.reshape(TOKENS, INNER).T
        for a in (
            spatial_query,
            spatial_key,
            spatial_value,
            temporal_query,
            temporal_key,
            temporal_value_in,
            out_grad,
        )
    )
    sq_gain, sk_gain, tq_gain, tk_gain = (
        g.reshape(1, HEAD_DIM)
        for g in (spatial_query_gain, spatial_key_gain, temporal_query_gain, temporal_key_gain)
    )
    seq = ("z", "y", "core")
    array = shape(INNER, TOKENS)
    args = (sq_gain, sk_gain, sq, sk, sv, tq, tk, og, tv_in)
    unit, inverse = shape(HEADS, HEAD_DIM, TOKENS, dtype=F32), shape(HEADS, 1, TOKENS, dtype=F32)
    normal, square = shape(HEADS, HEAD_DIM, TOKENS), shape(HEADS, 128, 128)
    sent, unit_q, unit_k, inverse_q, inverse_k, query, key_in, probs = call(
        send_kernel,
        (shape(2304, 128), unit, unit, inverse, inverse, normal, normal, shape(HEADS, 128, 128, dtype=F32)),
        *args,
        in_hbm=9,
        scratch=buffers(*args),
    )
    arrived = exchange(sent, seq, 18)
    args = (video_ids, tq_gain, tk_gain)
    sent, later, temporal = call(
        temporal_kernel,
        (shape(768, 128), shape(1536, 128), shape(HEAD_DIM, 1, dtype=F32)),
        arrived,
        *args,
        in_hbm=3,
        scratch=buffers(*args),
    )
    arrived = exchange(sent, seq, 6)
    grads_q, scores, gains = call(
        spatial_gain_kernel,
        (normal, square, shape(8, 2, 128, dtype=F32)),
        arrived,
        sv,
        unit_q,
        key_in,
        probs,
        temporal,
    )
    gains = lax.all_to_all(gains, ("dp", "core"), split_axis=0, concat_axis=0, tiled=True)
    ratios, message, out_early, grad_tv, grad_sq, grad_sk, grad_sv = call(
        spatial_rest_kernel,
        (shape(2, HEAD_DIM, dtype=F32), shape(1792, 128), shape(EARLY, TOKENS)) + (array,) * 4,
        arrived,
        later,
        unit_q,
        unit_k,
        inverse_q,
        inverse_k,
        query,
        probs,
        grads_q,
        scores,
        sq_gain,
        sk_gain,
        tq_gain,
        tk_gain,
        work=3_000_000_000,
    )
    sent = call(fill_kernel, shape(1792, 128), gains, message)
    arrived = exchange(sent, seq, 14)
    gain = shape(1, HEAD_DIM, dtype=F32)
    out, grad_tq, grad_tk, *gains = call(
        last_kernel,
        (array,) * 3 + (gain,) * 4,
        arrived,
        out_early,
        ratios,
    )
    results = (out, grad_sq, grad_sk, grad_sv, grad_tq, grad_tk, grad_tv)
    return tuple(a.T.reshape(1, 1, TOKENS, INNER) for a in results) + tuple(
        g.reshape(HEAD_DIM) for g in gains
    )


def solution(mesh):
    fine = Mesh(mesh.devices.reshape(4, 16, 4, 2), ("dp", "z", "y", "core"))
    tokens = P("dp", ("z", "y", "core"), None, None)
    return jax.shard_map(
        shards,
        mesh=fine,
        in_specs=(tokens,) * 7 + (P("dp", None),) + (P(),) * 4,
        out_specs=(tokens,) * 7 + (P(),) * 4,
        check_vma=False,
    )
```

```python
import jax
import jax.numpy as jnp
from jax import lax
from jax.experimental import pallas as pl
from jax.experimental.pallas import tpu as pltpu
from jax.sharding import Mesh
from jax.sharding import PartitionSpec as P

HEADS = 8
HEAD_DIM = 72
INNER = 576
TOKENS = 128
TILES = 18
ROWS = TILES * TOKENS
SCALE = HEAD_DIM ** (-0.5)
EPS = 1e-06
BF = jnp.bfloat16
F32 = jnp.float32
MIB = 1024 * 1024


def dot(left, right, left_dim, right_dim):
    return lax.dot_general(
        left, right, (((left_dim,), (right_dim,)), ((), ())), preferred_element_type=F32
    )


def pack(features, wide, out_ref):
    for tile in range(TILES):
        turned = features[128 * tile : 128 * tile + 128, :].T
        wide[pl.ds(tile, TOKENS, stride=TILES), :] = turned.astype(F32)
    out_ref[...] = wide[...].astype(BF)


def unpack(in_ref, wide, wanted=None):
    wide[...] = in_ref[...].astype(F32)
    tiles = [wide[pl.ds(tile, TOKENS, stride=TILES), :] for tile in range(wanted or TILES)]
    return jnp.concatenate([tile.astype(BF).T for tile in tiles], axis=0)


def column(gain_ref):
    row = lax.broadcasted_iota(jnp.int32, (HEAD_DIM, HEAD_DIM), 0)
    col = lax.broadcasted_iota(jnp.int32, (HEAD_DIM, HEAD_DIM), 1)
    spread = jnp.where(row == col, gain_ref[...], 0.0)
    return jnp.sum(spread, axis=1, keepdims=True)


def normed(values, gain):
    floats = values.astype(F32).reshape(HEADS, HEAD_DIM, TOKENS)
    inverse = lax.rsqrt(jnp.mean(floats * floats, axis=1, keepdims=True) + EPS)
    unit = floats * inverse
    return unit, inverse, (unit * gain[None]).astype(BF)


def normed_back(cotangent, unit, inverse, gain):
    scaled = cotangent * gain[None]
    along = jnp.mean(scaled * unit, axis=1, keepdims=True)
    return (inverse * (scaled - unit * along)).reshape(INNER, TOKENS).astype(BF)


def gain_terms(cotangent, unit):
    return jnp.sum(jnp.sum(cotangent * unit, axis=0), axis=1, keepdims=True)


def probabilities(query, key_in, same):
    products = [dot(key_in[h], query[h], 0, 0) for h in range(HEADS)]
    weights = [jnp.exp(product * SCALE) for product in products]
    if same is not None:
        weights = [weight * same for weight in weights]
    return [weight * (1.0 / jnp.sum(weight, axis=0, keepdims=True)) for weight in weights]


def scores_back(probs, grad_probs):
    along = [jnp.sum(p * g, axis=0, keepdims=True) for p, g in zip(probs, grad_probs)]
    return [(p * (g - a) * SCALE).astype(BF) for p, g, a in zip(probs, grad_probs, along)]


def heads(values):
    return [values[HEAD_DIM * h : HEAD_DIM * (h + 1), :] for h in range(HEADS)]


def dots(left, right, left_dim, right_dim):
    return [dot(left[h], right[h], left_dim, right_dim) for h in range(HEADS)]


def by_head(parts):
    return jnp.stack([part.astype(BF).astype(F32) for part in parts])


def load(sources, buffers, sems):
    copies = [
        pltpu.make_async_copy(source, buffer, sems.at[i])
        for i, (source, buffer) in enumerate(zip(sources, buffers))
    ]
    for copy in copies:
        copy.start()
    return copies


def send_kernel(*refs):
    sources, (out_ref, unit_q, unit_k, inverse_q, inverse_k, query, key_in, probs) = refs[:9], refs[9:17]
    wide, buffers, sems = refs[17], refs[18:-1], refs[-1]
    copies = load(sources, buffers, sems)
    gain_q, gain_k, sq, sk, sv, tq, tk, og, tv_in = buffers
    for copy in copies[:4]:
        copy.wait()
    unit_q[...], inverse_q[...], query[...] = normed(sq[...], column(gain_q))
    unit_k[...], inverse_k[...], key_in[...] = normed(sk[...], column(gain_k))
    for copy in copies[4:]:
        copy.wait()
    found = probabilities(query, key_in, None)
    for h in range(HEADS):
        probs[h] = found[h]
    mixed = dots(heads(sv), [p.astype(BF) for p in found], 1, 0)
    spatial = jnp.concatenate(mixed, axis=0).astype(BF)
    total = (tv_in[...].astype(F32) + spatial.astype(F32)).astype(BF)
    pack(jnp.concatenate([tq[...], tk[...], og[...], total], axis=0), wide, out_ref)


def same_video(ids):
    ids = jnp.broadcast_to(ids.astype(F32), (TOKENS, TOKENS))
    return (ids == ids.T).astype(F32)


def temporal_kernel(
    in_ref, ids_hbm, gain_q_hbm, gain_k_hbm, out_ref, gains_ref, wide, ids, gain_q, gain_k, sems
):
    copies = load((ids_hbm, gain_q_hbm, gain_k_hbm), (ids, gain_q, gain_k), sems)
    arrays = unpack(in_ref, wide)
    tq, tk, og, tv = (arrays[INNER * i : INNER * (i + 1), :] for i in range(4))
    for copy in copies:
        copy.wait()
    column_q, column_k = column(gain_q), column(gain_k)
    unit_q, inverse_q, query = normed(tq, column_q)
    unit_k, inverse_k, key_in = normed(tk, column_k)
    same = same_video(ids[...])
    values, cotangents = heads(tv), heads(og)
    probs = probabilities(query, key_in, same)
    grad_probs = dots(values, cotangents, 0, 0)
    rounded = [p.astype(BF) for p in probs]
    out = jnp.concatenate(dots(values, rounded, 1, 0), axis=0).astype(BF)
    grad_v = jnp.concatenate(dots(cotangents, rounded, 1, 1), axis=0).astype(BF)
    scores = scores_back(probs, grad_probs)
    grads_q = by_head(dots(key_in, scores, 1, 0))
    grads_k = by_head(dots(query, scores, 1, 1))
    gains_ref[...] = gain_terms(grads_q, unit_q)
    grad_q = normed_back(grads_q, unit_q, inverse_q, column_q)
    grad_k = normed_back(grads_k, unit_k, inverse_k, column_k)
    pack(jnp.concatenate([grad_v, out, grad_q, grad_k], axis=0), wide, out_ref)


def spatial_gain_kernel(in_ref, sv, unit_q, key_in, probs, temporal, grads_q, scores, out_ref, wide):
    given = unpack(in_ref, wide, 5)
    found = scores_back([probs[h] for h in range(HEADS)], dots(heads(sv), heads(given), 0, 0))
    products = [p.astype(BF) for p in dots(key_in, found, 1, 0)]
    for h in range(HEADS):
        scores[h] = found[h]
        grads_q[h] = products[h]
    total = gain_terms(by_head(products), unit_q[...])
    both = jnp.concatenate(
        [jnp.broadcast_to(t, (HEAD_DIM, 128)) for t in (total, temporal[...])], axis=0
    )
    both = jnp.concatenate([both, jnp.zeros((112, 128), F32)], axis=0)
    rows = jnp.concatenate([both[:128, :].T[:1, :], both[128:, :].T[:1, :]], axis=0)
    out_ref[...] = jnp.broadcast_to(rows[None], out_ref.shape)


def spatial_rest_kernel(
    in_ref, unit_q, unit_k, inverse_q, inverse_k, query, probs, grads_q, scores, gain_q, gain_k, gain_tq, gain_tk,
    ratios, out, grad_tq, grad_tk, grad_tv, grad_sq, grad_sk, grad_sv, wide
):
    ratios[...] = jnp.concatenate([gain_q[...] / gain_k[...], gain_tq[...] / gain_tk[...]], axis=0)
    arrays = unpack(in_ref, wide)
    grad_tv[...], out[...], grad_tq[...], grad_tk[...] = (
        arrays[INNER * i : INNER * (i + 1), :] for i in range(4)
    )
    grads_k = dots(query, scores, 1, 1)
    grads_v = dots(heads(arrays), [probs[h].astype(BF) for h in range(HEADS)], 1, 1)
    grad_sv[...] = jnp.concatenate(grads_v, axis=0).astype(BF)
    grad_sq[...] = normed_back(
        grads_q[...].astype(F32), unit_q[...], inverse_q[...], column(gain_q)
    )
    grad_sk[...] = normed_back(by_head(grads_k), unit_k[...], inverse_k[...], column(gain_k))


def gain_middle_kernel(in_ref, ratios, out_ref):
    out_ref[...] = jnp.broadcast_to(jnp.sum(in_ref[...], axis=0, keepdims=True), out_ref.shape)


def gain_last_kernel(in_ref, ratios, grad_sq, grad_sk, grad_tq, grad_tk):
    total = jnp.sum(in_ref[...], axis=0)
    spatial = total[:1, :HEAD_DIM]
    temporal = jnp.concatenate([total[:1, HEAD_DIM:], total[1:, : 2 * HEAD_DIM - 128]], axis=1)
    grad_sq[...] = spatial
    grad_sk[...] = spatial * ratios[:1, :]
    grad_tq[...] = temporal
    grad_tk[...] = temporal * ratios[1:, :]


def shape(*extent, dtype=BF):
    return jax.ShapeDtypeStruct(extent, dtype)


def call(kernel, out_shape, *args, in_hbm=0, scratch=(), work=0, vmem=32):
    specs = [pl.BlockSpec(memory_space=pltpu.VMEM)] * (len(args) - in_hbm)
    specs += [pl.BlockSpec(memory_space=pltpu.HBM)] * in_hbm
    split = len(args) - in_hbm
    args = args[:split] + tuple(
        pltpu.with_memory_space_constraint(a, pltpu.HBM) for a in args[split:]
    )
    cost = pl.CostEstimate(flops=work, bytes_accessed=0, transcendentals=0) if work else None
    return pl.pallas_call(
        kernel,
        out_shape=out_shape,
        in_specs=specs,
        scratch_shapes=scratch,
        compiler_params=pltpu.CompilerParams(vmem_limit_bytes=vmem * MIB),
        cost_estimate=cost,
    )(*args)


def buffers(*arrays):
    return [pltpu.VMEM(a.shape, a.dtype) for a in arrays] + [pltpu.SemaphoreType.DMA((len(arrays),))]


WIDE = [pltpu.VMEM((ROWS, 128), F32)]


def exchange(message):
    parts = message.reshape(TOKENS, TILES // 2, 2, 128)
    parts = lax.all_to_all(parts, ("z", "y", "core"), split_axis=0, concat_axis=0, tiled=True)
    return parts.reshape(ROWS, 128)


def shards(
    spatial_query,
    spatial_key,
    spatial_value,
    temporal_query,
    temporal_key,
    temporal_value_in,
    out_grad,
    video_ids,
    spatial_query_gain,
    spatial_key_gain,
    temporal_query_gain,
    temporal_key_gain,
):
    sq, sk, sv, tq, tk, tv_in, og = (
        a.reshape(TOKENS, INNER).T
        for a in (
            spatial_query,
            spatial_key,
            spatial_value,
            temporal_query,
            temporal_key,
            temporal_value_in,
            out_grad,
        )
    )
    sq_gain, sk_gain, tq_gain, tk_gain = (
        g.reshape(1, HEAD_DIM)
        for g in (spatial_query_gain, spatial_key_gain, temporal_query_gain, temporal_key_gain)
    )
    array = shape(INNER, TOKENS)
    args = (sq_gain, sk_gain, sq, sk, sv, tq, tk, og, tv_in)
    unit, inverse = shape(HEADS, HEAD_DIM, TOKENS, dtype=F32), shape(HEADS, 1, TOKENS, dtype=F32)
    normal, square = shape(HEADS, HEAD_DIM, TOKENS), shape(HEADS, 128, 128)
    sent, unit_q, unit_k, inverse_q, inverse_k, query, key_in, probs = call(
        send_kernel,
        (shape(ROWS, 128), unit, unit, inverse, inverse, normal, normal, shape(HEADS, 128, 128, dtype=F32)),
        *args,
        in_hbm=9,
        scratch=WIDE + buffers(*args),
    )
    arrived = exchange(sent)
    args = (video_ids, tq_gain, tk_gain)
    sent, temporal = call(
        temporal_kernel,
        (shape(ROWS, 128), shape(HEAD_DIM, 1, dtype=F32)),
        arrived,
        *args,
        in_hbm=3,
        scratch=WIDE + buffers(*args),
    )
    arrived = exchange(sent)
    grads_q, scores, gains = call(
        spatial_gain_kernel,
        (normal, square, shape(16, 2, 128, dtype=F32)),
        arrived,
        sv,
        unit_q,
        key_in,
        probs,
        temporal,
        scratch=WIDE,
    )
    gains = lax.all_to_all(gains, "z", split_axis=0, concat_axis=0, tiled=True)
    ratios, out, grad_tq, grad_tk, grad_tv, grad_sq, grad_sk, grad_sv = call(
        spatial_rest_kernel,
        (shape(2, HEAD_DIM, dtype=F32),) + (array,) * 7,
        arrived,
        unit_q,
        unit_k,
        inverse_q,
        inverse_k,
        query,
        probs,
        grads_q,
        scores,
        sq_gain,
        sk_gain,
        tq_gain,
        tk_gain,
        scratch=WIDE,
        work=3_000_000_000,
    )
    gains = call(gain_middle_kernel, shape(32, 2, 128, dtype=F32), gains, ratios)
    gains = lax.all_to_all(gains, ("core", "y", "dp"), split_axis=0, concat_axis=0, tiled=True)
    gains = call(gain_last_kernel, (shape(1, HEAD_DIM, dtype=F32),) * 4, gains, ratios)
    results = (out, grad_sq, grad_sk, grad_sv, grad_tq, grad_tk, grad_tv)
    return tuple(a.T.reshape(1, 1, TOKENS, INNER) for a in results) + tuple(
        g.reshape(HEAD_DIM) for g in gains
    )


def solution(mesh):
    fine = Mesh(mesh.devices.reshape(4, 16, 4, 2), ("dp", "z", "y", "core"))
    tokens = P("dp", ("z", "y", "core"), None, None)
    return jax.shard_map(
        shards,
        mesh=fine,
        in_specs=(tokens,) * 7 + (P("dp", None),) + (P(),) * 4,
        out_specs=(tokens,) * 7 + (P(),) * 4,
        check_vma=False,
    )
```

```python
import jax
import jax.numpy as jnp
from jax import lax
from jax.experimental import pallas as pl
from jax.experimental.pallas import tpu as pltpu
from jax.sharding import Mesh
from jax.sharding import PartitionSpec as P

HEADS = 8
HEAD_DIM = 72
INNER = 576
TOKENS = 128
TILES = 18
ROWS = TILES * TOKENS
SCALE = HEAD_DIM ** (-0.5)
EPS = 1e-06
BF = jnp.bfloat16
F32 = jnp.float32
MIB = 1024 * 1024


def dot(left, right, left_dim, right_dim):
    return lax.dot_general(
        left, right, (((left_dim,), (right_dim,)), ((), ())), preferred_element_type=F32
    )


def pack(features, wide, out_ref):
    for tile in range(TILES):
        turned = features[128 * tile : 128 * tile + 128, :].T
        wide[pl.ds(tile, TOKENS, stride=TILES), :] = turned.astype(F32)
    out_ref[...] = wide[...].astype(BF)


def unpack(in_ref, wide, wanted=None):
    wide[...] = in_ref[...].astype(F32)
    tiles = [wide[pl.ds(tile, TOKENS, stride=TILES), :] for tile in range(wanted or TILES)]
    return jnp.concatenate([tile.astype(BF).T for tile in tiles], axis=0)


def column(gain_ref):
    row = lax.broadcasted_iota(jnp.int32, (HEAD_DIM, HEAD_DIM), 0)
    col = lax.broadcasted_iota(jnp.int32, (HEAD_DIM, HEAD_DIM), 1)
    spread = jnp.where(row == col, gain_ref[...], 0.0)
    return jnp.sum(spread, axis=1, keepdims=True)


def normed(values, gain):
    floats = values.astype(F32).reshape(HEADS, HEAD_DIM, TOKENS)
    inverse = lax.rsqrt(jnp.mean(floats * floats, axis=1, keepdims=True) + EPS)
    unit = floats * inverse
    return unit, inverse, (unit * gain[None]).astype(BF)


def normed_back(cotangent, unit, inverse, gain):
    scaled = cotangent * gain[None]
    along = jnp.mean(scaled * unit, axis=1, keepdims=True)
    return (inverse * (scaled - unit * along)).reshape(INNER, TOKENS).astype(BF)


def gain_terms(cotangent, unit):
    return jnp.sum(cotangent * unit, axis=0)


def probabilities(query, key_in, same):
    products = [dot(key_in[h], query[h], 0, 0) for h in range(HEADS)]
    weights = [jnp.exp(product * SCALE) for product in products]
    if same is not None:
        weights = [weight * same for weight in weights]
    return [weight * (1.0 / jnp.sum(weight, axis=0, keepdims=True)) for weight in weights]


def scores_back(probs, grad_probs):
    along = [jnp.sum(p * g, axis=0, keepdims=True) for p, g in zip(probs, grad_probs)]
    return [(p * (g - a) * SCALE).astype(BF) for p, g, a in zip(probs, grad_probs, along)]


def heads(values):
    return [values[HEAD_DIM * h : HEAD_DIM * (h + 1), :] for h in range(HEADS)]


def dots(left, right, left_dim, right_dim):
    return [dot(left[h], right[h], left_dim, right_dim) for h in range(HEADS)]


def by_head(parts):
    return jnp.stack([part.astype(BF).astype(F32) for part in parts])


def load(sources, buffers, sems):
    copies = [
        pltpu.make_async_copy(source, buffer, sems.at[i])
        for i, (source, buffer) in enumerate(zip(sources, buffers))
    ]
    for copy in copies:
        copy.start()
    return copies


def send_kernel(*refs):
    sources, refs = refs[:12], refs[12:]
    out_ref, unit_q, unit_k, inverse_q, inverse_k, query, key_in, probs, gains, ratios, same = refs[:11]
    wide, buffers, sems = refs[11], refs[12:-1], refs[-1]
    copies = load(sources, buffers, sems)
    *rows, ids, sq, sk, sv, tq, tk, og, tv_in = buffers
    for copy in copies[:7]:
        copy.wait()
    for i in range(4):
        gains[i] = jnp.broadcast_to(column(rows[i]), (HEAD_DIM, TOKENS))
    ratios[...] = jnp.concatenate([rows[0][...] / rows[1][...], rows[2][...] / rows[3][...]], axis=0)
    same[...] = same_video(ids[...])
    unit_q[...], inverse_q[...], query[...] = normed(sq[...], gains[0])
    unit_k[...], inverse_k[...], key_in[...] = normed(sk[...], gains[1])
    found = probabilities(query, key_in, None)
    for copy in copies[7:]:
        copy.wait()
    for h in range(HEADS):
        probs[h] = found[h]
    mixed = dots(heads(sv), [p.astype(BF) for p in found], 1, 0)
    spatial = jnp.concatenate(mixed, axis=0).astype(BF)
    total = (tv_in[...].astype(F32) + spatial.astype(F32)).astype(BF)
    pack(jnp.concatenate([tq[...], tk[...], og[...], total], axis=0), wide, out_ref)


def same_video(ids):
    ids = jnp.broadcast_to(ids.astype(F32), (TOKENS, TOKENS))
    return (ids == ids.T).astype(F32)


def temporal_kernel(in_ref, gains, same, out_ref, terms_ref, wide):
    arrays = unpack(in_ref, wide)
    tq, tk, og, tv = (arrays[INNER * i : INNER * (i + 1), :] for i in range(4))
    unit_q, inverse_q, query = normed(tq, gains[2])
    unit_k, inverse_k, key_in = normed(tk, gains[3])
    values, cotangents = heads(tv), heads(og)
    probs = probabilities(query, key_in, same[...])
    grad_probs = dots(values, cotangents, 0, 0)
    rounded = [p.astype(BF) for p in probs]
    out = jnp.concatenate(dots(values, rounded, 1, 0), axis=0).astype(BF)
    grad_v = jnp.concatenate(dots(cotangents, rounded, 1, 1), axis=0).astype(BF)
    scores = scores_back(probs, grad_probs)
    grads_q = by_head(dots(key_in, scores, 1, 0))
    grads_k = by_head(dots(query, scores, 1, 1))
    terms_ref[...] = gain_terms(grads_q, unit_q)
    grad_q = normed_back(grads_q, unit_q, inverse_q, gains[2])
    grad_k = normed_back(grads_k, unit_k, inverse_k, gains[3])
    pack(jnp.concatenate([grad_v, out, grad_q, grad_k], axis=0), wide, out_ref)


def spatial_gain_kernel(in_ref, sv, unit_q, key_in, probs, temporal, grads_q, scores, out_ref, wide):
    given = unpack(in_ref, wide, 5)
    found = scores_back([probs[h] for h in range(HEADS)], dots(heads(sv), heads(given), 0, 0))
    products = [p.astype(BF) for p in dots(key_in, found, 1, 0)]
    for h in range(HEADS):
        scores[h] = found[h]
        grads_q[h] = products[h]
    total = gain_terms(by_head(products), unit_q[...])
    both = jnp.concatenate([total, temporal[...], jnp.zeros((112, 128), F32)], axis=0)
    rows = jnp.concatenate(
        [jnp.sum(part.T, axis=0, keepdims=True) for part in (both[:128, :], both[128:, :])], axis=0
    )
    out_ref[...] = jnp.broadcast_to(rows[None], out_ref.shape)


def spatial_rest_kernel(
    in_ref, unit_q, unit_k, inverse_q, inverse_k, query, probs, grads_q, scores, gains,
    out, grad_tq, grad_tk, grad_tv, grad_sq, grad_sk, grad_sv, wide
):
    arrays = unpack(in_ref, wide)
    grad_tv[...], out[...], grad_tq[...], grad_tk[...] = (
        arrays[INNER * i : INNER * (i + 1), :] for i in range(4)
    )
    grads_k = dots(query, scores, 1, 1)
    grads_v = dots(heads(arrays), [probs[h].astype(BF) for h in range(HEADS)], 1, 1)
    grad_sv[...] = jnp.concatenate(grads_v, axis=0).astype(BF)
    grad_sq[...] = normed_back(
        grads_q[...].astype(F32), unit_q[...], inverse_q[...], gains[0]
    )
    grad_sk[...] = normed_back(by_head(grads_k), unit_k[...], inverse_k[...], gains[1])


def gain_middle_kernel(in_ref, out_ref):
    out_ref[...] = jnp.broadcast_to(jnp.sum(in_ref[...], axis=0, keepdims=True), out_ref.shape)


def gain_last_kernel(in_ref, ratios, grad_sq, grad_sk, grad_tq, grad_tk):
    total = jnp.sum(in_ref[...], axis=0)
    spatial = total[:1, :HEAD_DIM]
    temporal = jnp.concatenate([total[:1, HEAD_DIM:], total[1:, : 2 * HEAD_DIM - 128]], axis=1)
    grad_sq[...] = spatial
    grad_sk[...] = spatial * ratios[:1, :]
    grad_tq[...] = temporal
    grad_tk[...] = temporal * ratios[1:, :]


def shape(*extent, dtype=BF):
    return jax.ShapeDtypeStruct(extent, dtype)


def call(kernel, out_shape, *args, in_hbm=0, scratch=(), work=0, vmem=32):
    specs = [pl.BlockSpec(memory_space=pltpu.VMEM)] * (len(args) - in_hbm)
    specs += [pl.BlockSpec(memory_space=pltpu.HBM)] * in_hbm
    split = len(args) - in_hbm
    args = args[:split] + tuple(
        pltpu.with_memory_space_constraint(a, pltpu.HBM) for a in args[split:]
    )
    cost = pl.CostEstimate(flops=work, bytes_accessed=0, transcendentals=0) if work else None
    return pl.pallas_call(
        kernel,
        out_shape=out_shape,
        in_specs=specs,
        scratch_shapes=scratch,
        compiler_params=pltpu.CompilerParams(vmem_limit_bytes=vmem * MIB),
        cost_estimate=cost,
    )(*args)


def buffers(*arrays):
    return [pltpu.VMEM(a.shape, a.dtype) for a in arrays] + [pltpu.SemaphoreType.DMA((len(arrays),))]


WIDE = [pltpu.VMEM((ROWS, 128), F32)]


def exchange(message):
    parts = message.reshape(TOKENS, TILES // 2, 2, 128)
    parts = lax.all_to_all(parts, ("z", "y", "core"), split_axis=0, concat_axis=0, tiled=True)
    return parts.reshape(ROWS, 128)


def shards(
    spatial_query,
    spatial_key,
    spatial_value,
    temporal_query,
    temporal_key,
    temporal_value_in,
    out_grad,
    video_ids,
    spatial_query_gain,
    spatial_key_gain,
    temporal_query_gain,
    temporal_key_gain,
):
    sq, sk, sv, tq, tk, tv_in, og = (
        a.reshape(TOKENS, INNER).T
        for a in (
            spatial_query,
            spatial_key,
            spatial_value,
            temporal_query,
            temporal_key,
            temporal_value_in,
            out_grad,
        )
    )
    sq_gain, sk_gain, tq_gain, tk_gain = (
        g.reshape(1, HEAD_DIM)
        for g in (spatial_query_gain, spatial_key_gain, temporal_query_gain, temporal_key_gain)
    )
    array = shape(INNER, TOKENS)
    args = (sq_gain, sk_gain, tq_gain, tk_gain, video_ids, sq, sk, sv, tq, tk, og, tv_in)
    unit, inverse = shape(HEADS, HEAD_DIM, TOKENS, dtype=F32), shape(HEADS, 1, TOKENS, dtype=F32)
    normal, square = shape(HEADS, HEAD_DIM, TOKENS), shape(HEADS, 128, 128)
    sent, unit_q, unit_k, inverse_q, inverse_k, query, key_in, probs, gain_columns, ratios, same = call(
        send_kernel,
        (
            shape(ROWS, 128),
            unit,
            unit,
            inverse,
            inverse,
            normal,
            normal,
            shape(HEADS, 128, 128, dtype=F32),
            shape(4, HEAD_DIM, TOKENS, dtype=F32),
            shape(2, HEAD_DIM, dtype=F32),
            shape(TOKENS, TOKENS, dtype=F32),
        ),
        *args,
        in_hbm=12,
        scratch=WIDE + buffers(*args),
    )
    arrived = exchange(sent)
    sent, temporal = call(
        temporal_kernel,
        (shape(ROWS, 128), shape(HEAD_DIM, TOKENS, dtype=F32)),
        arrived,
        gain_columns,
        same,
        scratch=WIDE,
    )
    arrived = exchange(sent)
    grads_q, scores, gains = call(
        spatial_gain_kernel,
        (normal, square, shape(16, 2, 128, dtype=F32)),
        arrived,
        sv,
        unit_q,
        key_in,
        probs,
        temporal,
        scratch=WIDE,
    )
    gains = lax.all_to_all(gains, "z", split_axis=0, concat_axis=0, tiled=True)
    out, grad_tq, grad_tk, grad_tv, grad_sq, grad_sk, grad_sv = call(
        spatial_rest_kernel,
        (array,) * 7,
        arrived,
        unit_q,
        unit_k,
        inverse_q,
        inverse_k,
        query,
        probs,
        grads_q,
        scores,
        gain_columns,
        scratch=WIDE,
        work=3_000_000_000,
    )
    gains = call(gain_middle_kernel, shape(32, 2, 128, dtype=F32), gains)
    gains = lax.all_to_all(gains, ("core", "y", "dp"), split_axis=0, concat_axis=0, tiled=True)
    gains = call(gain_last_kernel, (shape(1, HEAD_DIM, dtype=F32),) * 4, gains, ratios)
    results = (out, grad_sq, grad_sk, grad_sv, grad_tq, grad_tk, grad_tv)
    return tuple(a.T.reshape(1, 1, TOKENS, INNER) for a in results) + tuple(
        g.reshape(HEAD_DIM) for g in gains
    )


def solution(mesh):
    fine = Mesh(mesh.devices.reshape(4, 16, 4, 2), ("dp", "z", "y", "core"))
    tokens = P("dp", ("z", "y", "core"), None, None)
    return jax.shard_map(
        shards,
        mesh=fine,
        in_specs=(tokens,) * 7 + (P("dp", None),) + (P(),) * 4,
        out_specs=(tokens,) * 7 + (P(),) * 4,
        check_vma=False,
    )
```

```python
import jax
import jax.numpy as jnp
from jax import lax
from jax.experimental import pallas as pl
from jax.experimental.pallas import tpu as pltpu
from jax.sharding import Mesh
from jax.sharding import PartitionSpec as P

HEADS = 8
HEAD_DIM = 72
INNER = 576
TOKENS = 128
TILES = 18
ROWS = TILES * TOKENS
SCALE = HEAD_DIM ** (-0.5)
EPS = 1e-06
BF = jnp.bfloat16
F32 = jnp.float32
MIB = 1024 * 1024


def dot(left, right, left_dim, right_dim):
    return lax.dot_general(
        left, right, (((left_dim,), (right_dim,)), ((), ())), preferred_element_type=F32
    )


def pack(features, wide, out_ref):
    for tile in range(TILES):
        turned = features[128 * tile : 128 * tile + 128, :].T
        wide[pl.ds(tile, TOKENS, stride=TILES), :] = turned.astype(F32)
    out_ref[...] = wide[:ROWS, :].astype(BF)


def unpack(in_ref, wide, wanted=None):
    wide[:ROWS, :] = in_ref[...].astype(F32)
    tiles = [wide[pl.ds(tile, TOKENS, stride=TILES), :] for tile in range(wanted or TILES)]
    return jnp.concatenate([tile.astype(BF).T for tile in tiles], axis=0)


def column(gain_ref):
    row = lax.broadcasted_iota(jnp.int32, (HEAD_DIM, HEAD_DIM), 0)
    col = lax.broadcasted_iota(jnp.int32, (HEAD_DIM, HEAD_DIM), 1)
    spread = jnp.where(row == col, gain_ref[...], 0.0)
    return jnp.sum(spread, axis=1, keepdims=True)


def normed(values, gain):
    floats = values.astype(F32).reshape(HEADS, HEAD_DIM, TOKENS)
    inverse = lax.rsqrt(jnp.mean(floats * floats, axis=1, keepdims=True) + EPS)
    unit = floats * inverse
    return unit, inverse, (unit * gain[None]).astype(BF)


def normed_back(cotangent, unit, inverse, gain):
    scaled = cotangent * gain[None]
    along = jnp.mean(scaled * unit, axis=1, keepdims=True)
    return (inverse * (scaled - unit * along)).reshape(INNER, TOKENS).astype(BF)


def gain_terms(cotangent, unit):
    return jnp.sum(cotangent * unit, axis=0)


def probabilities(query, key_in, same):
    products = [dot(key_in[h], query[h], 0, 0) for h in range(HEADS)]
    weights = [jnp.exp(product * SCALE) for product in products]
    if same is not None:
        weights = [weight * same for weight in weights]
    return [weight * (1.0 / jnp.sum(weight, axis=0, keepdims=True)) for weight in weights]


def scores_back(probs, grad_probs):
    along = [jnp.sum(p * g, axis=0, keepdims=True) for p, g in zip(probs, grad_probs)]
    return [(p * (g - a) * SCALE).astype(BF) for p, g, a in zip(probs, grad_probs, along)]


def heads(values):
    return [values[HEAD_DIM * h : HEAD_DIM * (h + 1), :] for h in range(HEADS)]


def dots(left, right, left_dim, right_dim):
    return [dot(left[h], right[h], left_dim, right_dim) for h in range(HEADS)]


def by_head(parts):
    return jnp.stack([part.astype(BF).astype(F32) for part in parts])


def load(sources, buffers, sems):
    copies = [
        pltpu.make_async_copy(source, buffer, sems.at[i])
        for i, (source, buffer) in enumerate(zip(sources, buffers))
    ]
    for copy in copies:
        copy.start()
    return copies


def send_kernel(*refs):
    sources, refs = refs[:12], refs[12:]
    out_ref, unit_q, unit_k, inverse_q, inverse_k, query, key_in, probs, gains, ratios, same = refs[:11]
    wide, buffers, sems = refs[11], refs[12:-1], refs[-1]
    copies = load(sources, buffers, sems)
    *rows, ids, sq, sk, sv, tq, tk, og, tv_in = buffers
    for copy in copies[:5]:
        copy.wait()
    for i in range(4):
        gains[i] = jnp.broadcast_to(column(rows[i]), (HEAD_DIM, TOKENS))
    ratios[...] = jnp.concatenate([rows[0][...] / rows[1][...], rows[2][...] / rows[3][...]], axis=0)
    same[...] = same_video(ids[...])
    for copy in copies[5:7]:
        copy.wait()
    unit_q[...], inverse_q[...], query[...] = normed(sq[...], gains[0])
    unit_k[...], inverse_k[...], key_in[...] = normed(sk[...], gains[1])
    found = probabilities(query, key_in, None)
    for copy in copies[7:]:
        copy.wait()
    for h in range(HEADS):
        probs[h] = found[h]
    mixed = dots(heads(sv), [p.astype(BF) for p in found], 1, 0)
    spatial = jnp.concatenate(mixed, axis=0).astype(BF)
    total = (tv_in[...].astype(F32) + spatial.astype(F32)).astype(BF)
    pack(jnp.concatenate([tq[...], tk[...], og[...], total], axis=0), wide, out_ref)


def same_video(ids):
    ids = jnp.broadcast_to(ids.astype(F32), (TOKENS, TOKENS))
    return (ids == ids.T).astype(F32)


def temporal_kernel(in_ref, gains, same, out_ref, terms_ref, wide):
    arrays = unpack(in_ref, wide)
    tq, tk, og, tv = (arrays[INNER * i : INNER * (i + 1), :] for i in range(4))
    unit_q, inverse_q, query = normed(tq, gains[2])
    unit_k, inverse_k, key_in = normed(tk, gains[3])
    values, cotangents = heads(tv), heads(og)
    probs = probabilities(query, key_in, same[...])
    grad_probs = dots(values, cotangents, 0, 0)
    rounded = [p.astype(BF) for p in probs]
    out = jnp.concatenate(dots(values, rounded, 1, 0), axis=0).astype(BF)
    grad_v = jnp.concatenate(dots(cotangents, rounded, 1, 1), axis=0).astype(BF)
    scores = scores_back(probs, grad_probs)
    grads_q = by_head(dots(key_in, scores, 1, 0))
    grads_k = by_head(dots(query, scores, 1, 1))
    terms_ref[...] = gain_terms(grads_q, unit_q)
    grad_q = normed_back(grads_q, unit_q, inverse_q, gains[2])
    grad_k = normed_back(grads_k, unit_k, inverse_k, gains[3])
    pack(jnp.concatenate([grad_v, out, grad_q, grad_k], axis=0), wide, out_ref)


def spatial_gain_kernel(in_ref, sv, unit_q, key_in, probs, temporal, grads_q, scores, out_ref, wide):
    given = unpack(in_ref, wide, 5)
    found = scores_back([probs[h] for h in range(HEADS)], dots(heads(sv), heads(given), 0, 0))
    products = [p.astype(BF) for p in dots(key_in, found, 1, 0)]
    for h in range(HEADS):
        scores[h] = found[h]
        grads_q[h] = products[h]
    total = gain_terms(by_head(products), unit_q[...])
    both = jnp.concatenate([total, temporal[...], jnp.zeros((112, 128), F32)], axis=0)
    rows = jnp.concatenate(
        [jnp.sum(part.T, axis=0, keepdims=True) for part in (both[:128, :], both[128:, :])], axis=0
    )
    out_ref[...] = jnp.broadcast_to(rows[None], out_ref.shape)


def spatial_rest_kernel(
    in_ref, unit_q, unit_k, inverse_q, inverse_k, query, probs, grads_q, scores, gains,
    out, grad_tq, grad_tk, grad_tv, grad_sq, grad_sk, grad_sv, wide
):
    arrays = unpack(in_ref, wide)
    grad_tv[...], out[...], grad_tq[...], grad_tk[...] = (
        arrays[INNER * i : INNER * (i + 1), :] for i in range(4)
    )
    grads_k = dots(query, scores, 1, 1)
    grads_v = dots(heads(arrays), [probs[h].astype(BF) for h in range(HEADS)], 1, 1)
    grad_sv[...] = jnp.concatenate(grads_v, axis=0).astype(BF)
    grad_sq[...] = normed_back(
        grads_q[...].astype(F32), unit_q[...], inverse_q[...], gains[0]
    )
    grad_sk[...] = normed_back(by_head(grads_k), unit_k[...], inverse_k[...], gains[1])


def gain_middle_kernel(in_ref, out_ref):
    out_ref[...] = jnp.broadcast_to(jnp.sum(in_ref[...], axis=0, keepdims=True), out_ref.shape)


def gain_last_kernel(in_ref, ratios, grad_sq, grad_sk, grad_tq, grad_tk):
    total = jnp.sum(in_ref[...], axis=0)
    spatial = total[:1, :HEAD_DIM]
    temporal = jnp.concatenate([total[:1, HEAD_DIM:], total[1:, : 2 * HEAD_DIM - 128]], axis=1)
    grad_sq[...] = spatial
    grad_sk[...] = spatial * ratios[:1, :]
    grad_tq[...] = temporal
    grad_tk[...] = temporal * ratios[1:, :]


def shape(*extent, dtype=BF):
    return jax.ShapeDtypeStruct(extent, dtype)


def call(kernel, out_shape, *args, in_hbm=0, scratch=(), work=0, vmem=32):
    specs = [pl.BlockSpec(memory_space=pltpu.VMEM)] * (len(args) - in_hbm)
    specs += [pl.BlockSpec(memory_space=pltpu.HBM)] * in_hbm
    split = len(args) - in_hbm
    args = args[:split] + tuple(
        pltpu.with_memory_space_constraint(a, pltpu.HBM) for a in args[split:]
    )
    cost = pl.CostEstimate(flops=work, bytes_accessed=0, transcendentals=0) if work else None
    return pl.pallas_call(
        kernel,
        out_shape=out_shape,
        in_specs=specs,
        scratch_shapes=scratch,
        compiler_params=pltpu.CompilerParams(vmem_limit_bytes=vmem * MIB),
        cost_estimate=cost,
    )(*args)


def buffers(*arrays):
    return [pltpu.VMEM(a.shape, a.dtype) for a in arrays] + [pltpu.SemaphoreType.DMA((len(arrays),))]


WIDE = [pltpu.VMEM((ROWS + 24, 128), F32)]


def exchange(message):
    parts = message.reshape(TOKENS, TILES // 2, 2, 128)
    parts = lax.all_to_all(parts, ("z", "y", "core"), split_axis=0, concat_axis=0, tiled=True)
    return parts.reshape(ROWS, 128)


def shards(
    spatial_query,
    spatial_key,
    spatial_value,
    temporal_query,
    temporal_key,
    temporal_value_in,
    out_grad,
    video_ids,
    spatial_query_gain,
    spatial_key_gain,
    temporal_query_gain,
    temporal_key_gain,
):
    sq, sk, sv, tq, tk, tv_in, og = (
        a.reshape(TOKENS, INNER).T
        for a in (
            spatial_query,
            spatial_key,
            spatial_value,
            temporal_query,
            temporal_key,
            temporal_value_in,
            out_grad,
        )
    )
    sq_gain, sk_gain, tq_gain, tk_gain = (
        g.reshape(1, HEAD_DIM)
        for g in (spatial_query_gain, spatial_key_gain, temporal_query_gain, temporal_key_gain)
    )
    array = shape(INNER, TOKENS)
    args = (sq_gain, sk_gain, tq_gain, tk_gain, video_ids, sq, sk, sv, tq, tk, og, tv_in)
    unit, inverse = shape(HEADS, HEAD_DIM, TOKENS, dtype=F32), shape(HEADS, 1, TOKENS, dtype=F32)
    normal, square = shape(HEADS, HEAD_DIM, TOKENS), shape(HEADS, 128, 128)
    sent, unit_q, unit_k, inverse_q, inverse_k, query, key_in, probs, gain_columns, ratios, same = call(
        send_kernel,
        (
            shape(ROWS, 128),
            unit,
            unit,
            inverse,
            inverse,
            normal,
            normal,
            shape(HEADS, 128, 128, dtype=F32),
            shape(4, HEAD_DIM, TOKENS, dtype=F32),
            shape(2, HEAD_DIM, dtype=F32),
            shape(TOKENS, TOKENS, dtype=F32),
        ),
        *args,
        in_hbm=12,
        scratch=WIDE + buffers(*args),
    )
    arrived = exchange(sent)
    sent, temporal = call(
        temporal_kernel,
        (shape(ROWS, 128), shape(HEAD_DIM, TOKENS, dtype=F32)),
        arrived,
        gain_columns,
        same,
        scratch=WIDE,
    )
    arrived = exchange(sent)
    grads_q, scores, gains = call(
        spatial_gain_kernel,
        (normal, square, shape(16, 2, 128, dtype=F32)),
        arrived,
        sv,
        unit_q,
        key_in,
        probs,
        temporal,
        scratch=WIDE,
    )
    gains = lax.all_to_all(gains, "z", split_axis=0, concat_axis=0, tiled=True)
    out, grad_tq, grad_tk, grad_tv, grad_sq, grad_sk, grad_sv = call(
        spatial_rest_kernel,
        (array,) * 7,
        arrived,
        unit_q,
        unit_k,
        inverse_q,
        inverse_k,
        query,
        probs,
        grads_q,
        scores,
        gain_columns,
        scratch=WIDE,
        work=3_000_000_000,
    )
    gains = call(gain_middle_kernel, shape(32, 2, 128, dtype=F32), gains)
    gains = lax.all_to_all(gains, ("dp", "core", "y"), split_axis=0, concat_axis=0, tiled=True)
    gains = call(gain_last_kernel, (shape(1, HEAD_DIM, dtype=F32),) * 4, gains, ratios)
    results = (out, grad_sq, grad_sk, grad_sv, grad_tq, grad_tk, grad_tv)
    return tuple(a.T.reshape(1, 1, TOKENS, INNER) for a in results) + tuple(
        g.reshape(HEAD_DIM) for g in gains
    )


def solution(mesh):
    fine = Mesh(mesh.devices.reshape(4, 16, 4, 2), ("dp", "z", "y", "core"))
    tokens = P("dp", ("z", "y", "core"), None, None)
    return jax.shard_map(
        shards,
        mesh=fine,
        in_specs=(tokens,) * 7 + (P("dp", None),) + (P(),) * 4,
        out_specs=(tokens,) * 7 + (P(),) * 4,
        check_vma=False,
    )
```

```python
import jax
import jax.numpy as jnp
from jax import lax
from jax.experimental import pallas as pl
from jax.experimental.pallas import tpu as pltpu
from jax.sharding import Mesh
from jax.sharding import PartitionSpec as P

HEADS = 8
HEAD_DIM = 72
INNER = 576
TOKENS = 128
TILES = 18
ROWS = TILES * TOKENS
SCALE = HEAD_DIM ** (-0.5)
EPS = 1e-06
BF = jnp.bfloat16
F32 = jnp.float32
MIB = 1024 * 1024


def dot(left, right, left_dim, right_dim):
    return lax.dot_general(
        left, right, (((left_dim,), (right_dim,)), ((), ())), preferred_element_type=F32
    )


def pack(features, wide, out_ref):
    for tile in range(TILES):
        turned = features[128 * tile : 128 * tile + 128, :].T
        wide[pl.ds(tile, TOKENS, stride=TILES), :] = turned.astype(F32)
    out_ref[...] = wide[:ROWS, :].astype(BF)


def unpack(in_ref, wide, wanted=None):
    wide[:ROWS, :] = in_ref[...].astype(F32)
    tiles = [wide[pl.ds(tile, TOKENS, stride=TILES), :] for tile in range(wanted or TILES)]
    return jnp.concatenate([tile.astype(BF).T for tile in tiles], axis=0)


def column(gain_ref):
    row = lax.broadcasted_iota(jnp.int32, (HEAD_DIM, HEAD_DIM), 0)
    col = lax.broadcasted_iota(jnp.int32, (HEAD_DIM, HEAD_DIM), 1)
    spread = jnp.where(row == col, gain_ref[...], 0.0)
    return jnp.sum(spread, axis=1, keepdims=True)


def normed(values, gain):
    floats = values.astype(F32).reshape(HEADS, HEAD_DIM, TOKENS)
    inverse = lax.rsqrt(jnp.mean(floats * floats, axis=1, keepdims=True) + EPS)
    unit = floats * inverse
    return unit, inverse, (unit * gain[None]).astype(BF)


def normed_back(cotangent, unit, inverse, gain):
    scaled = cotangent * gain[None]
    along = jnp.mean(scaled * unit, axis=1, keepdims=True)
    return (inverse * (scaled - unit * along)).reshape(INNER, TOKENS).astype(BF)


def gain_terms(cotangent, unit):
    return jnp.sum(cotangent * unit, axis=0)


def probabilities(query, key_in, same):
    products = [dot(key_in[h], query[h], 0, 0) for h in range(HEADS)]
    weights = [jnp.exp(product * SCALE) for product in products]
    if same is not None:
        weights = [weight * same for weight in weights]
    return [weight * (1.0 / jnp.sum(weight, axis=0, keepdims=True)) for weight in weights]


def scores_back(probs, grad_probs):
    along = [jnp.sum(p * g, axis=0, keepdims=True) for p, g in zip(probs, grad_probs)]
    return [(p * (g - a) * SCALE).astype(BF) for p, g, a in zip(probs, grad_probs, along)]


def heads(values):
    return [values[HEAD_DIM * h : HEAD_DIM * (h + 1), :] for h in range(HEADS)]


def dots(left, right, left_dim, right_dim):
    return [dot(left[h], right[h], left_dim, right_dim) for h in range(HEADS)]


def by_head(parts):
    return jnp.stack([part.astype(BF).astype(F32) for part in parts])


def load(sources, buffers, sems):
    copies = [
        pltpu.make_async_copy(source, buffer, sems.at[i])
        for i, (source, buffer) in enumerate(zip(sources, buffers))
    ]
    for copy in copies:
        copy.start()
    return copies


def send_kernel(*refs):
    sources, refs = refs[:12], refs[12:]
    out_ref, unit_q, unit_k, inverse_q, inverse_k, query, key_in, probs, gains, ratios, same = refs[:11]
    wide, buffers, sems = refs[11], refs[12:-1], refs[-1]
    copies = load(sources, buffers, sems)
    *rows, ids, sq, sk, sv, tq, tk, og, tv_in = buffers
    for copy in copies[:5]:
        copy.wait()
    for i in range(4):
        gains[i] = jnp.broadcast_to(column(rows[i]), (HEAD_DIM, TOKENS))
    ratios[...] = jnp.concatenate([rows[0][...] / rows[1][...], rows[2][...] / rows[3][...]], axis=0)
    same[...] = same_video(ids[...])
    for copy in copies[5:7]:
        copy.wait()
    unit_q[...], inverse_q[...], query[...] = normed(sq[...], gains[0])
    unit_k[...], inverse_k[...], key_in[...] = normed(sk[...], gains[1])
    found = probabilities(query, key_in, None)
    for copy in copies[7:]:
        copy.wait()
    for h in range(HEADS):
        probs[h] = found[h]
    mixed = dots(heads(sv[...]), [p.astype(BF) for p in found], 1, 0)
    spatial = jnp.concatenate(mixed, axis=0).astype(BF)
    total = (tv_in[...].astype(F32) + spatial.astype(F32)).astype(BF)
    pack(jnp.concatenate([tq[...], tk[...], og[...], total], axis=0), wide, out_ref)


def same_video(ids):
    ids = jnp.broadcast_to(ids.astype(F32), (TOKENS, TOKENS))
    return (ids == ids.T).astype(F32)


def temporal_kernel(in_ref, gains, same, out_ref, terms_ref, wide):
    arrays = unpack(in_ref, wide)
    tq, tk, og, tv = (arrays[INNER * i : INNER * (i + 1), :] for i in range(4))
    unit_q, inverse_q, query = normed(tq, gains[2])
    unit_k, inverse_k, key_in = normed(tk, gains[3])
    values, cotangents = heads(tv), heads(og)
    probs = probabilities(query, key_in, same[...])
    grad_probs = dots(values, cotangents, 0, 0)
    rounded = [p.astype(BF) for p in probs]
    out = jnp.concatenate(dots(values, rounded, 1, 0), axis=0).astype(BF)
    grad_v = jnp.concatenate(dots(cotangents, rounded, 1, 1), axis=0).astype(BF)
    scores = scores_back(probs, grad_probs)
    grads_q = by_head(dots(key_in, scores, 1, 0))
    grads_k = by_head(dots(query, scores, 1, 1))
    terms_ref[...] = gain_terms(grads_q, unit_q)
    grad_q = normed_back(grads_q, unit_q, inverse_q, gains[2])
    grad_k = normed_back(grads_k, unit_k, inverse_k, gains[3])
    pack(jnp.concatenate([grad_v, out, grad_q, grad_k], axis=0), wide, out_ref)


def spatial_gain_kernel(in_ref, sv, unit_q, key_in, probs, temporal, grads_q, scores, out_ref, wide):
    given = unpack(in_ref, wide, 5)
    found = scores_back([probs[h] for h in range(HEADS)], dots(heads(sv[...]), heads(given), 0, 0))
    products = [p.astype(BF) for p in dots(key_in, found, 1, 0)]
    for h in range(HEADS):
        scores[h] = found[h]
        grads_q[h] = products[h]
    total = gain_terms(by_head(products), unit_q[...])
    both = jnp.concatenate([total, temporal[...], jnp.zeros((112, 128), F32)], axis=0)
    rows = jnp.concatenate(
        [jnp.sum(part.T, axis=0, keepdims=True) for part in (both[:128, :], both[128:, :])], axis=0
    )
    out_ref[...] = jnp.broadcast_to(rows[None], out_ref.shape)


def spatial_rest_kernel(
    in_ref, unit_q, unit_k, inverse_q, inverse_k, query, probs, grads_q, scores, gains,
    out, grad_tq, grad_tk, grad_tv, grad_sq, grad_sk, grad_sv, wide
):
    arrays = unpack(in_ref, wide)
    grad_tv[...], out[...], grad_tq[...], grad_tk[...] = (
        arrays[INNER * i : INNER * (i + 1), :] for i in range(4)
    )
    grads_k = dots(query, scores, 1, 1)
    grads_v = dots(heads(arrays), [probs[h].astype(BF) for h in range(HEADS)], 1, 1)
    grad_sv[...] = jnp.concatenate(grads_v, axis=0).astype(BF)
    grad_sq[...] = normed_back(
        grads_q[...].astype(F32), unit_q[...], inverse_q[...], gains[0]
    )
    grad_sk[...] = normed_back(by_head(grads_k), unit_k[...], inverse_k[...], gains[1])


def gain_middle_kernel(in_ref, out_ref):
    out_ref[...] = jnp.broadcast_to(jnp.sum(in_ref[...], axis=0, keepdims=True), out_ref.shape)


def gain_last_kernel(in_ref, ratios, grad_sq, grad_sk, grad_tq, grad_tk):
    total = jnp.sum(in_ref[...], axis=0)
    spatial = total[:1, :HEAD_DIM]
    temporal = jnp.concatenate([total[:1, HEAD_DIM:], total[1:, : 2 * HEAD_DIM - 128]], axis=1)
    grad_sq[...] = spatial
    grad_sk[...] = spatial * ratios[:1, :]
    grad_tq[...] = temporal
    grad_tk[...] = temporal * ratios[1:, :]


def shape(*extent, dtype=BF):
    return jax.ShapeDtypeStruct(extent, dtype)


def call(kernel, out_shape, *args, in_hbm=0, scratch=(), work=0, vmem=32):
    specs = [pl.BlockSpec(memory_space=pltpu.VMEM)] * (len(args) - in_hbm)
    specs += [pl.BlockSpec(memory_space=pltpu.HBM)] * in_hbm
    split = len(args) - in_hbm
    args = args[:split] + tuple(
        pltpu.with_memory_space_constraint(a, pltpu.HBM) for a in args[split:]
    )
    cost = pl.CostEstimate(flops=work, bytes_accessed=0, transcendentals=0) if work else None
    return pl.pallas_call(
        kernel,
        out_shape=out_shape,
        in_specs=specs,
        scratch_shapes=scratch,
        compiler_params=pltpu.CompilerParams(vmem_limit_bytes=vmem * MIB),
        cost_estimate=cost,
    )(*args)


def buffers(*arrays):
    return [pltpu.VMEM(a.shape, a.dtype) for a in arrays] + [pltpu.SemaphoreType.DMA((len(arrays),))]


WIDE = [pltpu.VMEM((ROWS + 24, 128), F32)]


def exchange(message):
    parts = message.reshape(TOKENS, TILES // 2, 2, 128)
    parts = lax.all_to_all(parts, ("z", "y", "core"), split_axis=0, concat_axis=0, tiled=True)
    return parts.reshape(ROWS, 128)


def shards(
    spatial_query,
    spatial_key,
    spatial_value,
    temporal_query,
    temporal_key,
    temporal_value_in,
    out_grad,
    video_ids,
    spatial_query_gain,
    spatial_key_gain,
    temporal_query_gain,
    temporal_key_gain,
):
    sq, sk, sv, tq, tk, tv_in, og = (
        a.reshape(TOKENS, INNER).T
        for a in (
            spatial_query,
            spatial_key,
            spatial_value,
            temporal_query,
            temporal_key,
            temporal_value_in,
            out_grad,
        )
    )
    sq_gain, sk_gain, tq_gain, tk_gain = (
        g.reshape(1, HEAD_DIM)
        for g in (spatial_query_gain, spatial_key_gain, temporal_query_gain, temporal_key_gain)
    )
    array = shape(INNER, TOKENS)
    args = (sq_gain, sk_gain, tq_gain, tk_gain, video_ids, sq, sk, sv, tq, tk, og, tv_in)
    unit, inverse = shape(HEADS, HEAD_DIM, TOKENS, dtype=F32), shape(HEADS, 1, TOKENS, dtype=F32)
    normal, square = shape(HEADS, HEAD_DIM, TOKENS), shape(HEADS, 128, 128)
    sent, unit_q, unit_k, inverse_q, inverse_k, query, key_in, probs, gain_columns, ratios, same = call(
        send_kernel,
        (
            shape(ROWS, 128),
            unit,
            unit,
            inverse,
            inverse,
            normal,
            normal,
            shape(HEADS, 128, 128, dtype=F32),
            shape(4, HEAD_DIM, TOKENS, dtype=F32),
            shape(2, HEAD_DIM, dtype=F32),
            shape(TOKENS, TOKENS, dtype=F32),
        ),
        *args,
        in_hbm=12,
        scratch=WIDE + buffers(*args),
    )
    arrived = exchange(sent)
    sent, temporal = call(
        temporal_kernel,
        (shape(ROWS, 128), shape(HEAD_DIM, TOKENS, dtype=F32)),
        arrived,
        gain_columns,
        same,
        scratch=WIDE,
    )
    arrived = exchange(sent)
    grads_q, scores, gains = call(
        spatial_gain_kernel,
        (normal, square, shape(16, 2, 128, dtype=F32)),
        arrived,
        sv,
        unit_q,
        key_in,
        probs,
        temporal,
        scratch=WIDE,
    )
    gains = lax.all_to_all(gains, "z", split_axis=0, concat_axis=0, tiled=True)
    out, grad_tq, grad_tk, grad_tv, grad_sq, grad_sk, grad_sv = call(
        spatial_rest_kernel,
        (array,) * 7,
        arrived,
        unit_q,
        unit_k,
        inverse_q,
        inverse_k,
        query,
        probs,
        grads_q,
        scores,
        gain_columns,
        scratch=WIDE,
        work=3_000_000_000,
    )
    gains = call(gain_middle_kernel, shape(32, 2, 128, dtype=F32), gains)
    gains = lax.all_to_all(gains, ("dp", "core", "y"), split_axis=0, concat_axis=0, tiled=True)
    gains = call(gain_last_kernel, (shape(1, HEAD_DIM, dtype=F32),) * 4, gains, ratios)
    results = (out, grad_sq, grad_sk, grad_sv, grad_tq, grad_tk, grad_tv)
    return tuple(a.T.reshape(1, 1, TOKENS, INNER) for a in results) + tuple(
        g.reshape(HEAD_DIM) for g in gains
    )


def solution(mesh):
    fine = Mesh(mesh.devices.reshape(4, 16, 4, 2), ("dp", "z", "y", "core"))
    tokens = P("dp", ("z", "y", "core"), None, None)
    return jax.shard_map(
        shards,
        mesh=fine,
        in_specs=(tokens,) * 7 + (P("dp", None),) + (P(),) * 4,
        out_specs=(tokens,) * 7 + (P(),) * 4,
        check_vma=False,
    )
```

```python
import jax
import jax.numpy as jnp
from jax import lax
from jax.experimental import pallas as pl
from jax.experimental.pallas import tpu as pltpu
from jax.sharding import Mesh
from jax.sharding import PartitionSpec as P

HEADS = 8
HEAD_DIM = 72
INNER = 576
TOKENS = 128
TILES = 18
ROWS = TILES * TOKENS
SCALE = HEAD_DIM ** (-0.5)
EPS = 1e-06
BF = jnp.bfloat16
F32 = jnp.float32
MIB = 1024 * 1024


def dot(left, right, left_dim, right_dim):
    return lax.dot_general(
        left, right, (((left_dim,), (right_dim,)), ((), ())), preferred_element_type=F32
    )


def pack(features, wide, out_ref):
    for tile in range(TILES):
        turned = features[128 * tile : 128 * tile + 128, :].T
        wide[pl.ds(tile, TOKENS, stride=TILES), :] = turned.astype(F32)
    out_ref[...] = wide[:ROWS, :].astype(BF)


def unpack(in_ref, wide, wanted=None):
    wide[:ROWS, :] = in_ref[...].astype(F32)
    tiles = [wide[pl.ds(tile, TOKENS, stride=TILES), :] for tile in range(wanted or TILES)]
    return jnp.concatenate([tile.astype(BF).T for tile in tiles], axis=0)


def column(gain_ref):
    row = lax.broadcasted_iota(jnp.int32, (HEAD_DIM, HEAD_DIM), 0)
    col = lax.broadcasted_iota(jnp.int32, (HEAD_DIM, HEAD_DIM), 1)
    spread = jnp.where(row == col, gain_ref[...], 0.0)
    return jnp.sum(spread, axis=1, keepdims=True)


def normed(values, gain):
    floats = values.astype(F32).reshape(HEADS, HEAD_DIM, TOKENS)
    inverse = lax.rsqrt(jnp.mean(floats * floats, axis=1, keepdims=True) + EPS)
    unit = floats * inverse
    return unit, inverse, (unit * gain[None]).astype(BF)


def normed_back(cotangent, unit, inverse, gain):
    scaled = cotangent * gain[None]
    along = jnp.mean(scaled * unit, axis=1, keepdims=True)
    return (inverse * (scaled - unit * along)).reshape(INNER, TOKENS).astype(BF)


def gain_terms(cotangent, unit):
    return jnp.sum(cotangent * unit, axis=0)


def probabilities(query, key_in, same):
    products = [dot(key_in[h], query[h], 0, 0) for h in range(HEADS)]
    weights = [jnp.exp(product * SCALE) for product in products]
    if same is not None:
        weights = [weight * same for weight in weights]
    return [weight * (1.0 / jnp.sum(weight, axis=0, keepdims=True)) for weight in weights]


def scores_back(probs, grad_probs):
    along = [jnp.sum(p * g, axis=0, keepdims=True) for p, g in zip(probs, grad_probs)]
    return [(p * (g - a) * SCALE).astype(BF) for p, g, a in zip(probs, grad_probs, along)]


def heads(values):
    return [values[HEAD_DIM * h : HEAD_DIM * (h + 1), :] for h in range(HEADS)]


def dots(left, right, left_dim, right_dim):
    return [dot(left[h], right[h], left_dim, right_dim) for h in range(HEADS)]


def by_head(parts):
    return jnp.stack([part.astype(BF).astype(F32) for part in parts])


def load(sources, buffers, sems):
    copies = [
        pltpu.make_async_copy(source, buffer, sems.at[i])
        for i, (source, buffer) in enumerate(zip(sources, buffers))
    ]
    for copy in copies:
        copy.start()
    return copies


def send_kernel(*refs):
    sources, refs = refs[:12], refs[12:]
    out_ref, unit_q, unit_k, inverse_q, inverse_k, query, key_in, probs, gains, ratios, same = refs[:11]
    wide, buffers, sems = refs[11], refs[12:-1], refs[-1]
    copies = load(sources, buffers, sems)
    *rows, ids, sq, sk, sv, tq, tk, og, tv_in = buffers
    for copy in copies[:5]:
        copy.wait()
    for i in range(4):
        gains[i] = jnp.broadcast_to(column(rows[i]), (HEAD_DIM, TOKENS))
    ratios[...] = jnp.concatenate([rows[0][...] / rows[1][...], rows[2][...] / rows[3][...]], axis=0)
    same[...] = same_video(ids[...])
    for copy in copies[5:7]:
        copy.wait()
    unit_q[...], inverse_q[...], query[...] = normed(sq[...], gains[0])
    unit_k[...], inverse_k[...], key_in[...] = normed(sk[...], gains[1])
    found = probabilities(query, key_in, None)
    for copy in copies[7:]:
        copy.wait()
    for h in range(HEADS):
        probs[h] = found[h]
    mixed = dots(heads(sv[...]), [p.astype(BF) for p in found], 1, 0)
    spatial = jnp.concatenate(mixed, axis=0).astype(BF)
    total = (tv_in[...].astype(F32) + spatial.astype(F32)).astype(BF)
    pack(jnp.concatenate([tq[...], tk[...], og[...], total], axis=0), wide, out_ref)


def same_video(ids):
    ids = jnp.broadcast_to(ids.astype(F32), (TOKENS, TOKENS))
    return (ids == ids.T).astype(F32)


def temporal_kernel(in_ref, gains, same, out_ref, terms_ref, wide):
    arrays = unpack(in_ref, wide)
    tq, tk, og, tv = (arrays[INNER * i : INNER * (i + 1), :] for i in range(4))
    unit_q, inverse_q, query = normed(tq, gains[2])
    unit_k, inverse_k, key_in = normed(tk, gains[3])
    values, cotangents = heads(tv), heads(og)
    probs = probabilities(query, key_in, same[...])
    grad_probs = dots(values, cotangents, 0, 0)
    rounded = [p.astype(BF) for p in probs]
    out = jnp.concatenate(dots(values, rounded, 1, 0), axis=0).astype(BF)
    grad_v = jnp.concatenate(dots(cotangents, rounded, 1, 1), axis=0).astype(BF)
    scores = scores_back(probs, grad_probs)
    grads_q = by_head(dots(key_in, scores, 1, 0))
    grads_k = by_head(dots(query, scores, 1, 1))
    terms_ref[...] = gain_terms(grads_q, unit_q)
    grad_q = normed_back(grads_q, unit_q, inverse_q, gains[2])
    grad_k = normed_back(grads_k, unit_k, inverse_k, gains[3])
    pack(jnp.concatenate([grad_v, out, grad_q, grad_k], axis=0), wide, out_ref)


def spatial_gain_kernel(in_ref, sv, unit_q, key_in, probs, temporal, grads_q, scores, out_ref, wide):
    given = unpack(in_ref, wide, 5)
    found = scores_back([probs[h] for h in range(HEADS)], dots(heads(sv[...]), heads(given), 0, 0))
    products = [p.astype(BF) for p in dots(key_in, found, 1, 0)]
    for h in range(HEADS):
        scores[h] = found[h]
        grads_q[h] = products[h]
    total = gain_terms(by_head(products), unit_q[...])
    both = jnp.concatenate([total, temporal[...], jnp.zeros((112, 128), F32)], axis=0)
    rows = jnp.concatenate(
        [jnp.sum(part.T, axis=0, keepdims=True) for part in (both[:128, :], both[128:, :])], axis=0
    )
    out_ref[...] = jnp.broadcast_to(rows[None], out_ref.shape)


def spatial_rest_kernel(*refs):
    in_ref, unit_q, unit_k, inverse_q, inverse_k, query, probs, grads_q, scores, gains, sums, ratios = refs[:12]
    targets, wide, results, sems = refs[12:23], refs[23], refs[24:35], refs[35]
    copies = [pltpu.make_async_copy(r, t, sems.at[i]) for i, (r, t) in enumerate(zip(results, targets))]
    out, grad_tq, grad_tk, grad_tv, grad_sq, grad_sk, grad_sv, *gain_grads = results
    gain_last_kernel(sums, ratios, *gain_grads)
    arrays = unpack(in_ref, wide)
    grad_tv[...], out[...], grad_tq[...], grad_tk[...] = (
        arrays[INNER * i : INNER * (i + 1), :] for i in range(4)
    )
    for copy in copies[:4] + copies[7:]:
        copy.start()
    grads_k = dots(query, scores, 1, 1)
    grads_v = dots(heads(arrays), [probs[h].astype(BF) for h in range(HEADS)], 1, 1)
    grad_sv[...] = jnp.concatenate(grads_v, axis=0).astype(BF)
    copies[6].start()
    grad_sq[...] = normed_back(
        grads_q[...].astype(F32), unit_q[...], inverse_q[...], gains[0]
    )
    copies[4].start()
    grad_sk[...] = normed_back(by_head(grads_k), unit_k[...], inverse_k[...], gains[1])
    copies[5].start()
    for copy in copies:
        copy.wait()


def gain_middle_kernel(in_ref, out_ref):
    out_ref[...] = jnp.broadcast_to(jnp.sum(in_ref[...], axis=0, keepdims=True), out_ref.shape)


def gain_last_kernel(in_ref, ratios, grad_sq, grad_sk, grad_tq, grad_tk):
    total = jnp.sum(in_ref[...], axis=0)
    spatial = total[:1, :HEAD_DIM]
    temporal = jnp.concatenate([total[:1, HEAD_DIM:], total[1:, : 2 * HEAD_DIM - 128]], axis=1)
    grad_sq[...] = spatial
    grad_sk[...] = spatial * ratios[:1, :]
    grad_tq[...] = temporal
    grad_tk[...] = temporal * ratios[1:, :]


def shape(*extent, dtype=BF):
    return jax.ShapeDtypeStruct(extent, dtype)


def call(kernel, out_shape, *args, in_hbm=0, scratch=(), work=0, vmem=32, out_hbm=False):
    specs = [pl.BlockSpec(memory_space=pltpu.VMEM)] * (len(args) - in_hbm)
    specs += [pl.BlockSpec(memory_space=pltpu.HBM)] * in_hbm
    split = len(args) - in_hbm
    args = args[:split] + tuple(
        pltpu.with_memory_space_constraint(a, pltpu.HBM) for a in args[split:]
    )
    cost = pl.CostEstimate(flops=work, bytes_accessed=0, transcendentals=0) if work else None
    out_space = pltpu.HBM if out_hbm else pltpu.VMEM
    return pl.pallas_call(
        kernel,
        out_shape=out_shape,
        out_specs=jax.tree.map(lambda _: pl.BlockSpec(memory_space=out_space), out_shape),
        in_specs=specs,
        scratch_shapes=scratch,
        compiler_params=pltpu.CompilerParams(vmem_limit_bytes=vmem * MIB),
        cost_estimate=cost,
    )(*args)


def buffers(*arrays):
    return [pltpu.VMEM(a.shape, a.dtype) for a in arrays] + [pltpu.SemaphoreType.DMA((len(arrays),))]


WIDE = [pltpu.VMEM((ROWS + 24, 128), F32)]


def exchange(message):
    parts = message.reshape(TOKENS, TILES // 2, 2, 128)
    parts = lax.all_to_all(parts, ("z", "y", "core"), split_axis=0, concat_axis=0, tiled=True)
    return parts.reshape(ROWS, 128)


def shards(
    spatial_query,
    spatial_key,
    spatial_value,
    temporal_query,
    temporal_key,
    temporal_value_in,
    out_grad,
    video_ids,
    spatial_query_gain,
    spatial_key_gain,
    temporal_query_gain,
    temporal_key_gain,
):
    sq, sk, sv, tq, tk, tv_in, og = (
        a.reshape(TOKENS, INNER).T
        for a in (
            spatial_query,
            spatial_key,
            spatial_value,
            temporal_query,
            temporal_key,
            temporal_value_in,
            out_grad,
        )
    )
    sq_gain, sk_gain, tq_gain, tk_gain = (
        g.reshape(1, HEAD_DIM)
        for g in (spatial_query_gain, spatial_key_gain, temporal_query_gain, temporal_key_gain)
    )
    array = shape(INNER, TOKENS)
    args = (sq_gain, sk_gain, tq_gain, tk_gain, video_ids, sq, sk, sv, tq, tk, og, tv_in)
    unit, inverse = shape(HEADS, HEAD_DIM, TOKENS, dtype=F32), shape(HEADS, 1, TOKENS, dtype=F32)
    normal, square = shape(HEADS, HEAD_DIM, TOKENS), shape(HEADS, 128, 128)
    sent, unit_q, unit_k, inverse_q, inverse_k, query, key_in, probs, gain_columns, ratios, same = call(
        send_kernel,
        (
            shape(ROWS, 128),
            unit,
            unit,
            inverse,
            inverse,
            normal,
            normal,
            shape(HEADS, 128, 128, dtype=F32),
            shape(4, HEAD_DIM, TOKENS, dtype=F32),
            shape(2, HEAD_DIM, dtype=F32),
            shape(TOKENS, TOKENS, dtype=F32),
        ),
        *args,
        in_hbm=12,
        scratch=WIDE + buffers(*args),
    )
    arrived = exchange(sent)
    sent, temporal = call(
        temporal_kernel,
        (shape(ROWS, 128), shape(HEAD_DIM, TOKENS, dtype=F32)),
        arrived,
        gain_columns,
        same,
        scratch=WIDE,
    )
    arrived = exchange(sent)
    grads_q, scores, gains = call(
        spatial_gain_kernel,
        (normal, square, shape(16, 2, 128, dtype=F32)),
        arrived,
        sv,
        unit_q,
        key_in,
        probs,
        temporal,
        scratch=WIDE,
    )
    gains = lax.all_to_all(gains, "z", split_axis=0, concat_axis=0, tiled=True)
    gains = call(gain_middle_kernel, shape(32, 2, 128, dtype=F32), gains)
    gains = lax.all_to_all(gains, ("dp", "core", "y"), split_axis=0, concat_axis=0, tiled=True)
    rest = (array,) * 7 + (shape(1, HEAD_DIM, dtype=F32),) * 4
    out, grad_tq, grad_tk, grad_tv, grad_sq, grad_sk, grad_sv, *gains = call(
        spatial_rest_kernel,
        rest,
        arrived,
        unit_q,
        unit_k,
        inverse_q,
        inverse_k,
        query,
        probs,
        grads_q,
        scores,
        gain_columns,
        gains,
        ratios,
        scratch=WIDE + [pltpu.VMEM(r.shape, r.dtype) for r in rest] + [pltpu.SemaphoreType.DMA((11,))],
        out_hbm=True,
    )
    results = (out, grad_sq, grad_sk, grad_sv, grad_tq, grad_tk, grad_tv)
    return tuple(a.T.reshape(1, 1, TOKENS, INNER) for a in results) + tuple(
        g.reshape(HEAD_DIM) for g in gains
    )


def solution(mesh):
    fine = Mesh(mesh.devices.reshape(4, 16, 4, 2), ("dp", "z", "y", "core"))
    tokens = P("dp", ("z", "y", "core"), None, None)
    return jax.shard_map(
        shards,
        mesh=fine,
        in_specs=(tokens,) * 7 + (P("dp", None),) + (P(),) * 4,
        out_specs=(tokens,) * 7 + (P(),) * 4,
        check_vma=False,
    )
```

```python
import jax
import jax.numpy as jnp
from jax import lax
from jax.experimental import pallas as pl
from jax.experimental.pallas import tpu as pltpu
from jax.sharding import Mesh
from jax.sharding import PartitionSpec as P

HEADS = 8
HEAD_DIM = 72
INNER = 576
TOKENS = 128
TILES = 18
ROWS = TILES * TOKENS
SCALE = HEAD_DIM ** (-0.5)
EPS = 1e-06
BF = jnp.bfloat16
F32 = jnp.float32
MIB = 1024 * 1024


def dot(left, right, left_dim, right_dim):
    return lax.dot_general(
        left, right, (((left_dim,), (right_dim,)), ((), ())), preferred_element_type=F32
    )


def pack(features, wide, out_ref):
    for tile in range(TILES):
        turned = features[128 * tile : 128 * tile + 128, :].T
        wide[pl.ds(tile, TOKENS, stride=TILES), :] = turned.astype(F32)
    out_ref[...] = wide[:ROWS, :].astype(BF)


def unpack(in_ref, wide, wanted=None):
    wide[:ROWS, :] = in_ref[...].astype(F32)
    tiles = [wide[pl.ds(tile, TOKENS, stride=TILES), :] for tile in range(wanted or TILES)]
    return jnp.concatenate([tile.astype(BF).T for tile in tiles], axis=0)


def column(gain_ref):
    row = lax.broadcasted_iota(jnp.int32, (HEAD_DIM, HEAD_DIM), 0)
    col = lax.broadcasted_iota(jnp.int32, (HEAD_DIM, HEAD_DIM), 1)
    spread = jnp.where(row == col, gain_ref[...], 0.0)
    return jnp.sum(spread, axis=1, keepdims=True)


def normed(values, gain):
    floats = values.astype(F32).reshape(HEADS, HEAD_DIM, TOKENS)
    inverse = lax.rsqrt(jnp.mean(floats * floats, axis=1, keepdims=True) + EPS)
    unit = floats * inverse
    return unit, inverse, (unit * gain[None]).astype(BF)


def normed_back(cotangent, unit, inverse, gain):
    scaled = cotangent * gain[None]
    along = jnp.mean(scaled * unit, axis=1, keepdims=True)
    return (inverse * (scaled - unit * along)).reshape(INNER, TOKENS).astype(BF)


def gain_terms(cotangent, unit):
    return jnp.sum(cotangent * unit, axis=0)


def probabilities(query, key_in, same):
    products = [dot(key_in[h], query[h], 0, 0) for h in range(HEADS)]
    weights = [jnp.exp(product * SCALE) for product in products]
    if same is not None:
        weights = [weight * same for weight in weights]
    return [weight * (1.0 / jnp.sum(weight, axis=0, keepdims=True)) for weight in weights]


def scores_back(probs, grad_probs):
    along = [jnp.sum(p * g, axis=0, keepdims=True) for p, g in zip(probs, grad_probs)]
    return [(p * (g - a) * SCALE).astype(BF) for p, g, a in zip(probs, grad_probs, along)]


def heads(values):
    return [values[HEAD_DIM * h : HEAD_DIM * (h + 1), :] for h in range(HEADS)]


def dots(left, right, left_dim, right_dim):
    return [dot(left[h], right[h], left_dim, right_dim) for h in range(HEADS)]


def by_head(parts):
    return jnp.stack([part.astype(BF).astype(F32) for part in parts])


def load(sources, buffers, sems):
    copies = [
        pltpu.make_async_copy(source, buffer, sems.at[i])
        for i, (source, buffer) in enumerate(zip(sources, buffers))
    ]
    for copy in copies:
        copy.start()
    return copies


def send_kernel(*refs):
    sources, refs = refs[:12], refs[12:]
    out_ref, unit_q, unit_k, inverse_q, inverse_k, query, key_in, probs, gains, ratios, same = refs[:11]
    wide, buffers, sems = refs[11], refs[12:-1], refs[-1]
    copies = load(sources, buffers, sems)
    *rows, ids, sq, sk, sv, tq, tk, og, tv_in = buffers
    for copy in copies[:5]:
        copy.wait()
    for i in range(4):
        gains[i] = jnp.broadcast_to(column(rows[i]), (HEAD_DIM, TOKENS))
    ratios[...] = jnp.concatenate([rows[0][...] / rows[1][...], rows[2][...] / rows[3][...]], axis=0)
    same[...] = same_video(ids[...])
    for copy in copies[5:7]:
        copy.wait()
    unit_q[...], inverse_q[...], query[...] = normed(sq[...], gains[0])
    unit_k[...], inverse_k[...], key_in[...] = normed(sk[...], gains[1])
    found = probabilities(query, key_in, None)
    for copy in copies[7:]:
        copy.wait()
    for h in range(HEADS):
        probs[h] = found[h]
    mixed = dots(heads(sv[...]), [p.astype(BF) for p in found], 1, 0)
    spatial = jnp.concatenate(mixed, axis=0).astype(BF)
    total = (tv_in[...].astype(F32) + spatial.astype(F32)).astype(BF)
    pack(jnp.concatenate([tq[...], tk[...], og[...], total], axis=0), wide, out_ref)


def same_video(ids):
    ids = jnp.broadcast_to(ids.astype(F32), (TOKENS, TOKENS))
    return (ids == ids.T).astype(F32)


def temporal_kernel(in_ref, gains, same, out_ref, terms_ref, wide):
    arrays = unpack(in_ref, wide)
    tq, tk, og, tv = (arrays[INNER * i : INNER * (i + 1), :] for i in range(4))
    unit_q, inverse_q, query = normed(tq, gains[2])
    unit_k, inverse_k, key_in = normed(tk, gains[3])
    values, cotangents = heads(tv), heads(og)
    probs = probabilities(query, key_in, same[...])
    grad_probs = dots(values, cotangents, 0, 0)
    rounded = [p.astype(BF) for p in probs]
    out = jnp.concatenate(dots(values, rounded, 1, 0), axis=0).astype(BF)
    grad_v = jnp.concatenate(dots(cotangents, rounded, 1, 1), axis=0).astype(BF)
    scores = scores_back(probs, grad_probs)
    grads_q = by_head(dots(key_in, scores, 1, 0))
    grads_k = by_head(dots(query, scores, 1, 1))
    terms_ref[...] = gain_terms(grads_q, unit_q)
    grad_q = normed_back(grads_q, unit_q, inverse_q, gains[2])
    grad_k = normed_back(grads_k, unit_k, inverse_k, gains[3])
    pack(jnp.concatenate([grad_v, out, grad_q, grad_k], axis=0), wide, out_ref)


def spatial_gain_kernel(in_ref, sv, unit_q, key_in, probs, temporal, grads_q, scores, out_ref, wide):
    given = unpack(in_ref, wide, 5)
    found = scores_back([probs[h] for h in range(HEADS)], dots(heads(sv[...]), heads(given), 0, 0))
    products = [p.astype(BF) for p in dots(key_in, found, 1, 0)]
    for h in range(HEADS):
        scores[h] = found[h]
        grads_q[h] = products[h]
    total = gain_terms(by_head(products), unit_q[...])
    both = jnp.concatenate([total, temporal[...], jnp.zeros((112, 128), F32)], axis=0)
    rows = jnp.concatenate(
        [jnp.sum(part.T, axis=0, keepdims=True) for part in (both[:128, :], both[128:, :])], axis=0
    )
    out_ref[...] = jnp.broadcast_to(rows[None], out_ref.shape)


def spatial_rest_kernel(
    in_ref, unit_q, unit_k, inverse_q, inverse_k, query, probs, grads_q, scores, gains, sums, ratios,
    out, grad_tq, grad_tk, grad_tv, grad_sq, grad_sk, grad_sv, gain_sq, gain_sk, gain_tq, gain_tk, wide
):
    gain_last_kernel(sums, ratios, gain_sq, gain_sk, gain_tq, gain_tk)
    arrays = unpack(in_ref, wide)
    grad_tv[...], out[...], grad_tq[...], grad_tk[...] = (
        arrays[INNER * i : INNER * (i + 1), :] for i in range(4)
    )
    grads_k = dots(query, scores, 1, 1)
    grads_v = dots(heads(arrays), [probs[h].astype(BF) for h in range(HEADS)], 1, 1)
    grad_sv[...] = jnp.concatenate(grads_v, axis=0).astype(BF)
    grad_sq[...] = normed_back(
        grads_q[...].astype(F32), unit_q[...], inverse_q[...], gains[0]
    )
    grad_sk[...] = normed_back(by_head(grads_k), unit_k[...], inverse_k[...], gains[1])


def gain_middle_kernel(in_ref, out_ref):
    out_ref[...] = jnp.broadcast_to(jnp.sum(in_ref[...], axis=0, keepdims=True), out_ref.shape)


def gain_last_kernel(in_ref, ratios, grad_sq, grad_sk, grad_tq, grad_tk):
    total = jnp.sum(in_ref[...], axis=0)
    spatial = total[:1, :HEAD_DIM]
    temporal = jnp.concatenate([total[:1, HEAD_DIM:], total[1:, : 2 * HEAD_DIM - 128]], axis=1)
    grad_sq[...] = spatial
    grad_sk[...] = spatial * ratios[:1, :]
    grad_tq[...] = temporal
    grad_tk[...] = temporal * ratios[1:, :]


def shape(*extent, dtype=BF):
    return jax.ShapeDtypeStruct(extent, dtype)


def call(kernel, out_shape, *args, in_hbm=0, scratch=(), work=0, vmem=32):
    specs = [pl.BlockSpec(memory_space=pltpu.VMEM)] * (len(args) - in_hbm)
    specs += [pl.BlockSpec(memory_space=pltpu.HBM)] * in_hbm
    split = len(args) - in_hbm
    args = args[:split] + tuple(
        pltpu.with_memory_space_constraint(a, pltpu.HBM) for a in args[split:]
    )
    cost = pl.CostEstimate(flops=work, bytes_accessed=0, transcendentals=0) if work else None
    return pl.pallas_call(
        kernel,
        out_shape=out_shape,
        in_specs=specs,
        scratch_shapes=scratch,
        compiler_params=pltpu.CompilerParams(vmem_limit_bytes=vmem * MIB),
        cost_estimate=cost,
    )(*args)


def buffers(*arrays):
    return [pltpu.VMEM(a.shape, a.dtype) for a in arrays] + [pltpu.SemaphoreType.DMA((len(arrays),))]


WIDE = [pltpu.VMEM((ROWS + 24, 128), F32)]


def exchange(message):
    parts = message.reshape(TOKENS, TILES // 2, 2, 128)
    parts = lax.all_to_all(parts, ("z", "y", "core"), split_axis=0, concat_axis=0, tiled=True)
    return parts.reshape(ROWS, 128)


def shards(
    spatial_query,
    spatial_key,
    spatial_value,
    temporal_query,
    temporal_key,
    temporal_value_in,
    out_grad,
    video_ids,
    spatial_query_gain,
    spatial_key_gain,
    temporal_query_gain,
    temporal_key_gain,
):
    sq, sk, sv, tq, tk, tv_in, og = (
        a.reshape(TOKENS, INNER).T
        for a in (
            spatial_query,
            spatial_key,
            spatial_value,
            temporal_query,
            temporal_key,
            temporal_value_in,
            out_grad,
        )
    )
    sq_gain, sk_gain, tq_gain, tk_gain = (
        g.reshape(1, HEAD_DIM)
        for g in (spatial_query_gain, spatial_key_gain, temporal_query_gain, temporal_key_gain)
    )
    array = shape(INNER, TOKENS)
    args = (sq_gain, sk_gain, tq_gain, tk_gain, video_ids, sq, sk, sv, tq, tk, og, tv_in)
    unit, inverse = shape(HEADS, HEAD_DIM, TOKENS, dtype=F32), shape(HEADS, 1, TOKENS, dtype=F32)
    normal, square = shape(HEADS, HEAD_DIM, TOKENS), shape(HEADS, 128, 128)
    sent, unit_q, unit_k, inverse_q, inverse_k, query, key_in, probs, gain_columns, ratios, same = call(
        send_kernel,
        (
            shape(ROWS, 128),
            unit,
            unit,
            inverse,
            inverse,
            normal,
            normal,
            shape(HEADS, 128, 128, dtype=F32),
            shape(4, HEAD_DIM, TOKENS, dtype=F32),
            shape(2, HEAD_DIM, dtype=F32),
            shape(TOKENS, TOKENS, dtype=F32),
        ),
        *args,
        in_hbm=12,
        scratch=WIDE + buffers(*args),
    )
    arrived = exchange(sent)
    sent, temporal = call(
        temporal_kernel,
        (shape(ROWS, 128), shape(HEAD_DIM, TOKENS, dtype=F32)),
        arrived,
        gain_columns,
        same,
        scratch=WIDE,
    )
    arrived = exchange(sent)
    grads_q, scores, gains = call(
        spatial_gain_kernel,
        (normal, square, shape(16, 2, 128, dtype=F32)),
        arrived,
        sv,
        unit_q,
        key_in,
        probs,
        temporal,
        scratch=WIDE,
    )
    gains = lax.all_to_all(gains, "z", split_axis=0, concat_axis=0, tiled=True)
    gains = call(gain_middle_kernel, shape(32, 2, 128, dtype=F32), gains)
    gains = lax.all_to_all(gains, ("dp", "core", "y"), split_axis=0, concat_axis=0, tiled=True)
    out, grad_tq, grad_tk, grad_tv, grad_sq, grad_sk, grad_sv, *gains = call(
        spatial_rest_kernel,
        (array,) * 7 + (shape(1, HEAD_DIM, dtype=F32),) * 4,
        arrived,
        unit_q,
        unit_k,
        inverse_q,
        inverse_k,
        query,
        probs,
        grads_q,
        scores,
        gain_columns,
        gains,
        ratios,
        scratch=WIDE,
    )
    results = (out, grad_sq, grad_sk, grad_sv, grad_tq, grad_tk, grad_tv)
    return tuple(a.T.reshape(1, 1, TOKENS, INNER) for a in results) + tuple(
        g.reshape(HEAD_DIM) for g in gains
    )


def solution(mesh):
    fine = Mesh(mesh.devices.reshape(4, 16, 4, 2), ("dp", "z", "y", "core"))
    tokens = P("dp", ("z", "y", "core"), None, None)
    return jax.shard_map(
        shards,
        mesh=fine,
        in_specs=(tokens,) * 7 + (P("dp", None),) + (P(),) * 4,
        out_specs=(tokens,) * 7 + (P(),) * 4,
        check_vma=False,
    )
```
